128 devices in a mesh: flow: 32 (over y, z, core), grp: 4 (over x).
Axes of the slice: x: 4, y: 4, z: 4, core: 2. Of those that a mesh axis runs over, the one named last changes fastest.
Arguments:
- fluid_point_warmth: float32 [512, 131072], P(None, ('flow', 'grp')), may hold values from -6 to 6
- velocity: float32 [512, 131072], P(None, ('flow', 'grp')), may hold values from 0.3 to 1.2
- wall_film: float32 [128, 131072], P(None, ('flow', 'grp')), may hold values from 0.5 to 5
- face_owner: int32 [262144, 1], P(('flow', 'grp')), may hold values from 0 to 127; in each aligned block of 2048 rows (0 to 2047, 2048 to 4095, ...) at most 32 rows name the same one
- plate_temp: float32 [128, 65536], P(None, ('flow', 'grp')), may hold values from -6 to 6
- conductivity: float32 [128, 65536], P(None, ('flow', 'grp')), may hold values from 0.25 to 2
- plate_cell: int32 [524288], P(('flow', 'grp')), may hold values from 0 to 511
Outputs:
- coolant_out: float32 [512, 131072], P(None, ('flow', 'grp'))
- boundary_sheet_warmth: float32 [128, 131072], P(None, ('flow', 'grp'))
- sheet_conducted_warmth: float32 [128, 65536], P(None, ('flow', 'grp'))
The draws below stay inside these ranges and needn't reach their ends.
Inputs may be any that keep to these rules, and one draw needn't show every extreme that they name: `face_owner`: among the 2048 faces of one device at most 32 name the same owner, and that bound is reached.
All inputs are finite; a program needn't handle non-finite values.
Results may differ from the reference program's by a relative error of at most 0.0001.
Values sent between devices are 32-bit elements; how exact they have to be, the bound alone decides.
No kernel may reach another device: no remote copies, remote signals or barrier semaphores. Data moves between devices by JAX's collectives and lax.ppermute only.
A program may use at most 64 MiB of HBM per device.

```python
import math
import jax
import jax.numpy as jnp
import numpy as np
from jax import lax

P_DEV = 512
PTS = 512
SWEEPS = 2
E = 131072
W_DEV = 2048
CAP = 32
SLOTS = 4096
P_SIZE = 65536
N_FLOW = 32
N_GRP = 4


def place_ends(values, own_key, low, largest):
    shape = values.shape
    spot = [jax.random.randint(jax.random.fold_in(own_key, axis), (), 0, shape[axis]) for axis in range(len(shape))]
    values = values.at[tuple(spot)].set(low)
    longest = shape.index(max(shape))
    spot[longest] = (spot[longest] + 1) % shape[longest]
    return values.at[tuple(spot)].set(largest)


def block_scale(stream_key, shape, cuts, low, high):
    level = 1.0
    for dim, parts in cuts:
        heights = jax.random.uniform(jax.random.fold_in(jax.random.fold_in(stream_key, 6), dim), (parts,), jnp.float32, low / len(cuts), high / len(cuts))
        level = level * jnp.repeat(jnp.exp(heights), shape[dim] // parts).reshape((-1,) + (1,) * (len(shape) - 1 - dim))
    return level


def shared_out(own_key, own, number, rows, amount, top, limit, skew):
    sequence = jax.random.permutation(own_key, amount)
    crowded, common = load_shares(amount, rows * top, limit, skew, True), load_shares(amount, rows * top, limit, skew, False)
    places = jnp.arange(amount)

    def named(tallies, offset_by):
        used = int((tallies > 0).sum())
        fixed = max(1, used // 4)
        passed = fixed + (places - fixed + offset_by * (used - fixed)) % max(1, amount - fixed)
        return jnp.zeros((amount,), jnp.int32).at[sequence[jnp.where(places < fixed, places, passed)]].set(jnp.asarray(tallies, jnp.int32))

    tallies = jnp.where(number % 4 == 0, named(crowded, number // 4), named(common, number - number // 4 - 1))
    mixed = jax.random.permutation(jax.random.fold_in(own, 3), amount)
    giver, taker = mixed[0:amount // 2 * 2:2], mixed[1:amount // 2 * 2:2]
    room = jnp.minimum(tallies[giver] - 1, limit - tallies[taker]) // 2
    room = jnp.where((giver == sequence[0]) | (taker == sequence[0]) | (tallies[taker] == 0), 0, jnp.maximum(room, 0))
    passed = jax.random.randint(jax.random.fold_in(own, 4), (amount // 2,), 0, 1 << 20) % (room + 1)
    tallies = tallies.at[giver].add(-passed).at[taker].add(passed)
    items = jnp.searchsorted(jnp.cumsum(tallies), jnp.arange(rows * top), side="right").astype(jnp.int32)
    listing = items.reshape(top, rows).T
    listing = listing[jax.random.permutation(jax.random.fold_in(own, 1), rows)]
    offset_by = jax.random.randint(jax.random.fold_in(own, 2), (rows, 1), 0, top)
    return jnp.take_along_axis(listing, (jnp.arange(top)[None, :] + offset_by) % top, axis=1)


def load_shares(count, total, reach, slope, full):
    loads = [(1 << 20) // math.isqrt(rank ** slope) + 1 for rank in range(1, count + 1)]
    largest = reach if full else min(reach, max(-(-total // count), total * loads[0] // sum(loads)))
    least = 1 if total - largest >= count - 1 else 0
    holding, rest = [largest] + [least] * (count - 1), total - largest - least * (count - 1)
    while rest > 0:
        candidates = [i for i in range(1, count) if holding[i] < largest] or [i for i in range(1, count) if holding[i] < reach]
        mass, remaining = sum([loads[i] for i in candidates]), rest
        for i in candidates:
            more = min(reach - holding[i], max(1, remaining * loads[i] // mass), rest)
            holding[i] = holding[i] + more
            rest = rest - more
    return np.array(holding)


def bell_draw(own_key, extent, scale, bound, cuts=(), kind=jnp.bfloat16):
    values = scale * jax.random.normal(own_key, extent, jnp.float32)
    if cuts:
        values = values * block_scale(own_key, extent, cuts, -0.22, 0.18)
    return jnp.clip(values, -bound, bound).astype(kind)


def setup_inputs(seed: int = 0) -> dict:
    streams_of = jax.random.split(jax.random.key(seed), 8)
    fluid_point_warmth = bell_draw(streams_of[0], (PTS, E), 1.0, 6.0, ((1, 128),), jnp.float32)
    velocity = jnp.clip(0.3 + 0.90000004 * jax.random.uniform(streams_of[1], (PTS, E), jnp.float32) ** block_scale(streams_of[1], (PTS, E), ((1, 128),), -0.2, 0.2), 0.3, 1.2)
    wall_film = jnp.clip(jnp.exp(math.log(5.0) - 2.3025851 * jax.random.uniform(streams_of[2], (128, E), jnp.float32) ** block_scale(streams_of[2], (128, E), ((1, 128),), -0.2, 0.2)), 0.5, 5.0)
    face_owner_keys = jax.random.split(jax.random.fold_in(streams_of[3], 1), (2 * E) // W_DEV)
    face_owner_turns = jax.random.permutation(jax.random.fold_in(streams_of[3], 3), (2 * E) // W_DEV)
    face_owner = jax.vmap(lambda own, number: shared_out(jax.random.fold_in(streams_of[3], 2), own, number, W_DEV, N_FLOW * N_GRP, 1, CAP, 2))(face_owner_keys, face_owner_turns).reshape((2 * E, 1))
    plate_temp = bell_draw(streams_of[4], (128, P_SIZE), 1.0, 6.0, ((1, 128),), jnp.float32)
    conductivity = jnp.clip(jnp.exp(math.log(2.0) - 2.0794415 * jax.random.uniform(streams_of[5], (128, P_SIZE), jnp.float32) ** block_scale(streams_of[5], (128, P_SIZE), ((1, 128),), -0.2, 0.2)), 0.25, 2.0)
    plate_cell = place_ends(jax.random.randint(streams_of[6], (N_FLOW * N_GRP * SLOTS,), 0, P_DEV), jax.random.fold_in(streams_of[6], 1), 0, P_DEV - 1).astype(jnp.int32)
    return dict(fluid_point_warmth=fluid_point_warmth, velocity=velocity, wall_film=wall_film, face_owner=face_owner, plate_temp=plate_temp, conductivity=conductivity, plate_cell=plate_cell)


LAMBDA_H = 4.0
DAMPING_RATIO = 0.5
CARRY_STEP_SIZE = 0.05
CONTACT = 0.1
DT_PLATE = 0.0008
COUPLE = 20.0
MIXING_WEIGHT = 0.5
GLL_POINTS = (-1.0, -0.8717401485096066, -0.5917001814331423, -0.2092992179024789, 0.2092992179024789, 0.5917001814331423, 0.8717401485096066, 1.0)
GLL_WEIGHTS = (0.03571428571428571, 0.2107042271435061, 0.3411226924835044, 0.4124587946587038, 0.4124587946587038, 0.3411226924835044, 0.2107042271435061, 0.03571428571428571)


def gll_tables():
    points = np.array(GLL_POINTS)
    weights = np.array(GLL_WEIGHTS)
    number = points.shape[0]
    identity = np.eye(number)
    spread = points[:, None] - points[None, :] + identity
    bary_weight = 1.0 / np.prod(spread, axis=1)
    pointwise_gradient = (bary_weight[None, :] / bary_weight[:, None]) / spread
    pointwise_gradient = pointwise_gradient * (1.0 - identity)
    pointwise_gradient = pointwise_gradient - identity * pointwise_gradient.sum(axis=1)[:, None]
    stiffness = (pointwise_gradient.T * weights[None, :]) @ pointwise_gradient
    stiff_diag = np.sum(stiffness * identity, axis=1)
    weight_matrix = identity * weights[None, :]
    wa = weights[:, None, None]
    wb = weights[None, :, None]
    wc = weights[None, None, :]
    main_entry_mass = LAMBDA_H * wa * wb * wc + stiff_diag[:, None, None] * wb * wc + wa * stiff_diag[None, :, None] * wc + wa * wb * stiff_diag[None, None, :]
    in_plane = (np.kron(stiffness, weight_matrix) + np.kron(weight_matrix, stiffness)) / np.kron(weights, weights)[:, None]
    through = np.array([[-1.0, 1.0], [1.0, -1.0]])
    plate_op = -np.kron(np.eye(2), in_plane) + COUPLE * np.kron(through, np.eye(64))
    return (jnp.asarray(pointwise_gradient, jnp.float32), jnp.asarray(weights, jnp.float32), jnp.asarray(stiffness, jnp.float32), jnp.asarray(main_entry_mass, jnp.float32), jnp.asarray(plate_op, jnp.float32))


def matrix_per_direction(matrix, field, axis_number):
    einsum_forms = ("ij,jbce->ibce", "ij,ajce->aice", "ij,abje->abie")
    return jnp.einsum(einsum_forms[axis_number], matrix, field, precision=lax.Precision.HIGHEST)


def stiff_apply(field, weights, stiffness):
    wa = weights[:, None, None, None]
    wb = weights[None, :, None, None]
    wc = weights[None, None, :, None]
    return matrix_per_direction(stiffness, field, 0) * wb * wc + matrix_per_direction(stiffness, field, 1) * wa * wc + matrix_per_direction(stiffness, field, 2) * wa * wb


def reference(fluid_point_warmth, velocity, wall_film, face_owner, plate_temp, conductivity, plate_cell):
    pointwise_gradient, weights, stiffness, main_entry_mass, plate_op = gll_tables()
    overall_count = fluid_point_warmth.shape[1]
    pointwise_warmth = fluid_point_warmth.reshape(8, 8, 8, overall_count)
    speed_mass_product = velocity.reshape(8, 8, 8, overall_count)
    element = jnp.arange(overall_count, dtype=jnp.int32)
    inner_low = (element > 0).astype(jnp.float32)
    inner_high = (element < overall_count - 1).astype(jnp.float32)
    main_entry_aggregate = jnp.broadcast_to(main_entry_mass[..., None], pointwise_warmth.shape)
    main_entry_aggregate = main_entry_aggregate.at[0].add(main_entry_mass[7][..., None] * inner_low).at[7].add(main_entry_mass[0][..., None] * inner_high)
    zero_face = jnp.zeros((8, 8, 1), jnp.float32)
    for sweep_step in range(SWEEPS):
        carried_quantity = pointwise_warmth - CARRY_STEP_SIZE * speed_mass_product * matrix_per_direction(pointwise_gradient, pointwise_warmth, 0)
        residual = -stiff_apply(carried_quantity, weights, stiffness)
        prev_high = jnp.concatenate([zero_face, residual[7][..., :-1]], -1)
        next_low = jnp.concatenate([residual[0][..., 1:], zero_face], -1)
        collapsed_aggregate = residual.at[0].add(prev_high).at[7].add(next_low)
        pointwise_warmth = carried_quantity + DAMPING_RATIO * collapsed_aggregate / main_entry_aggregate
    boundary_rate_aggregate = 2 * overall_count
    barrier_warmth = jnp.stack([pointwise_warmth[:, 0].reshape(64, overall_count), pointwise_warmth[:, 7].reshape(64, overall_count)], -1).reshape(64, boundary_rate_aggregate)
    layer_records = jnp.stack([wall_film[:64], wall_film[64:]], -1).reshape(64, boundary_rate_aggregate)
    devices = N_FLOW * N_GRP
    target = face_owner[:, 0]
    source = jnp.arange(boundary_rate_aggregate, dtype=jnp.int32) // W_DEV
    onehot = (target.reshape(devices, W_DEV, 1) == jnp.arange(devices, dtype=jnp.int32)[None, None, :]).astype(jnp.int32)
    earlier = jnp.cumsum(onehot, axis=1) - onehot
    slot_rank = jnp.sum(earlier * onehot, axis=-1).reshape(boundary_rate_aggregate)
    slot_global = target * SLOTS + source * CAP + slot_rank
    element_entire = target * P_DEV + jnp.take(plate_cell, slot_global, axis=0)
    sheet_aggregate = plate_temp.shape[1]
    film_sum = jax.ops.segment_sum(layer_records.T, element_entire, sheet_aggregate).T
    thermal_energy_accumulated = jax.ops.segment_sum((layer_records * barrier_warmth).T, element_entire, sheet_aggregate).T
    contact = (plate_temp[:64] + CONTACT * thermal_energy_accumulated) / (1.0 + CONTACT * film_sum)
    relaxed = jnp.concatenate([contact, plate_temp[64:]], 0)
    sheet_conducted_warmth = relaxed + DT_PLATE * conductivity * jnp.dot(plate_op, relaxed, precision=lax.Precision.HIGHEST)
    touching_boundary = jnp.take(sheet_conducted_warmth[:64], element_entire, axis=1)
    yielded_energy = (layer_records * (touching_boundary - barrier_warmth)).reshape(64, overall_count, 2)
    contact_back = touching_boundary.reshape(64, overall_count, 2)
    pointwise_warmth = pointwise_warmth.at[:, 0].add(MIXING_WEIGHT * yielded_energy[..., 0].reshape(8, 8, overall_count))
    pointwise_warmth = pointwise_warmth.at[:, 7].add(MIXING_WEIGHT * yielded_energy[..., 1].reshape(8, 8, overall_count))
    boundary_sheet_warmth = jnp.concatenate([contact_back[..., 0], contact_back[..., 1]], 0)
    return pointwise_warmth.reshape(512, overall_count), boundary_sheet_warmth, sheet_conducted_warmth
```

```python
import functools

import jax
import jax.numpy as jnp
import ml_dtypes
import numpy as np
from jax import lax
from jax.experimental import pallas as pl
from jax.experimental.pallas import tpu as pltpu
from jax.sharding import PartitionSpec as P

SWEEPS = 2
LAMBDA_H = 4.0
DAMPING_RATIO = 0.5
CARRY_STEP_SIZE = 0.05
CONTACT = 0.1
DT_PLATE = 0.0008
COUPLE = 20.0
MIXING_WEIGHT = 0.5
GLL_POINTS = (
    -1.0,
    -0.8717401485096066,
    -0.5917001814331423,
    -0.2092992179024789,
    0.2092992179024789,
    0.5917001814331423,
    0.8717401485096066,
    1.0,
)
GLL_WEIGHTS = (
    0.03571428571428571,
    0.2107042271435061,
    0.3411226924835044,
    0.4124587946587038,
    0.4124587946587038,
    0.3411226924835044,
    0.2107042271435061,
    0.03571428571428571,
)
LANES = 128
VMEM_LIMIT = 56 * 1024 * 1024


def split_pair(table):
    high = np.asarray(table, np.float32).astype(ml_dtypes.bfloat16)
    low = (np.asarray(table, np.float64) - high.astype(np.float64)).astype(np.float32)
    return high, low.astype(ml_dtypes.bfloat16)


def gll_tables():
    points = np.array(GLL_POINTS)
    weights = np.array(GLL_WEIGHTS)
    identity = np.eye(8)
    spread = points[:, None] - points[None, :] + identity
    bary_weight = 1.0 / np.prod(spread, axis=1)
    gradient = bary_weight[None, :] / bary_weight[:, None] / spread
    gradient = gradient * (1.0 - identity)
    gradient = gradient - identity * gradient.sum(axis=1)[:, None]
    stiffness = gradient.T * weights[None, :] @ gradient
    strong = stiffness / weights[:, None]
    ratio = np.diag(strong)
    laplace = (
        np.kron(np.kron(strong, identity), identity)
        + np.kron(np.kron(identity, strong), identity)
        + np.kron(np.kron(identity, identity), strong)
    )
    diagonal = (
        LAMBDA_H + ratio[:, None, None] + ratio[None, :, None] + ratio[None, None, :]
    ).reshape(512)
    share = np.ones((8, 64))
    share[0] = 0.5
    share[7] = 0.5
    smooth = -DAMPING_RATIO * (share.reshape(512) / diagonal)[:, None] * laplace
    quad = smooth.reshape(8, 64, 8, 64)
    near = quad[:4, :, :4, :]
    far = quad[:4, :, 7:3:-1, :]
    even = (0.5 * (near + far)).reshape(256, 256)
    odd = (0.5 * (near - far)).reshape(256, 256)
    carry = -CARRY_STEP_SIZE * gradient
    from_even = 0.5 * (carry[:4, :4] + carry[:4, 7:3:-1])
    from_odd = 0.5 * (carry[:4, :4] - carry[:4, 7:3:-1])
    weight_matrix = np.diag(weights)
    in_plane = (np.kron(stiffness, weight_matrix) + np.kron(weight_matrix, stiffness)) / np.kron(
        weights, weights
    )[:, None]
    through = np.array([[-1.0, 1.0], [1.0, -1.0]])
    plate_op = -np.kron(np.eye(2), in_plane) + COUPLE * np.kron(through, np.eye(64))
    even_parts = split_pair(even)
    odd_parts = split_pair(odd)
    smoothing = np.stack(
        [np.concatenate(even_parts, 1), np.concatenate(odd_parts, 1)]
    )
    plate_parts = np.concatenate(split_pair(plate_op), 1)
    return from_even, from_odd, smoothing, plate_parts


def halves(value):
    high = value.astype(jnp.bfloat16)
    low = (value - high.astype(jnp.float32)).astype(jnp.bfloat16)
    return high, low


def dot32(a, b):
    return jnp.dot(a, b, preferred_element_type=jnp.float32)


def edge_kernel(t_low, t_high, v_low, v_high, to_next, to_prev):
    tl = t_low[...].T
    vl = v_low[...].T
    th = t_high[...].T
    vh = v_high[...].T
    to_prev[0:2, :] = tl[0:2, :]
    to_prev[2:4, :] = vl[0:2, :]
    to_prev[4:8, :] = jnp.zeros((4, 512), jnp.float32)
    to_next[0:2, :] = th[126:128, :]
    to_next[2:4, :] = vh[126:128, :]
    to_next[4:8, :] = jnp.zeros((4, 512), jnp.float32)


def rank_kernel(owner, position):
    wide = 256
    row = lax.broadcasted_iota(jnp.int32, (wide, wide), 0)
    col = lax.broadcasted_iota(jnp.int32, (wide, wide), 1)
    upto = (row <= col).astype(jnp.float32).astype(jnp.bfloat16)
    name = lax.broadcasted_iota(jnp.int32, (128, LANES), 0)
    before = jnp.zeros((128, 1), jnp.float32)
    for step in range(8):
        pair = [
            (name == owner[2 * step + i : 2 * step + i + 1, :]).astype(jnp.float32)
            for i in range(2)
        ]
        hot = jnp.concatenate(pair, axis=1)
        seen = dot32(hot.astype(jnp.bfloat16), upto)
        rank = jnp.sum(hot * (seen + before), axis=0, keepdims=True) - 1.0
        before = before + seen[:, wide - 1 : wide]
        for i in range(2):
            at = slice(2 * step + i, 2 * step + i + 1)
            position[at, :] = owner[at, :] * 32 + rank[:, i * LANES : (i + 1) * LANES].astype(
                jnp.int32
            )


def sweep_kernel(
    from_even,
    from_odd,
    ends,
    t_in,
    v_in,
    film,
    from_prev,
    from_next,
    smoothing,
    position,
    t_out,
    wall_out,
    sending,
    tx,
    vx,
    adv,
    high,
    low,
    even,
    odd,
    edge,
    faces,
    sems,
    out_sems,
):
    count = t_in.shape[-1]
    blocks = count // LANES + 1
    loads = []
    for b in range(8):
        pair = (
            pltpu.make_async_copy(t_in.at[:, b], tx.at[:, b, :, pl.ds(0, count)], sems.at[0, b]),
            pltpu.make_async_copy(v_in.at[:, b], vx.at[:, b, :, pl.ds(0, count)], sems.at[1, b]),
        )
        for copy in pair:
            copy.start()
        loads.append(pair)
    edge[...] = jnp.zeros_like(edge)
    edge[0:2, :] = from_next[0:2, :]
    edge[126:128, :] = from_prev[0:2, :]
    tx[:, :, :, pl.ds(count, LANES)] = edge[...].T.reshape(8, 8, 8, LANES)
    edge[0:2, :] = from_next[2:4, :]
    edge[126:128, :] = from_prev[2:4, :]
    vx[:, :, :, pl.ds(count, LANES)] = edge[...].T.reshape(8, 8, 8, LANES)
    sending[...] = jnp.zeros_like(sending)
    lane = lax.broadcasted_iota(jnp.int32, (8, LANES), 1)
    is_first = ends[0] == 1
    is_last = ends[1] == 1

    def carry(pair, lanes):
        at = pl.ds(2 * pair, 2)
        t = [tx[a, at, :, lanes].reshape(16, LANES) for a in range(8)]
        v = [vx[a, at, :, lanes].reshape(16, LANES) for a in range(8)]
        e = [t[k] + t[7 - k] for k in range(4)]
        o = [t[k] - t[7 - k] for k in range(4)]
        for i in range(4):
            p = sum(float(from_even[i, j]) * e[j] for j in range(4))
            q = sum(float(from_odd[i, j]) * o[j] for j in range(4))
            near = t[i] + v[i] * (q + p)
            far = t[7 - i] + v[7 - i] * (q - p)
            adv[i, at, :, lanes] = near.reshape(2, 8, LANES)
            adv[7 - i, at, :, lanes] = far.reshape(2, 8, LANES)
            for number, part in enumerate((near + far, near - far)):
                first, second = halves(part)
                rows = pl.ds(256 * number + 64 * i + 16 * pair, 16)
                high[rows, lanes] = first
                low[rows, lanes] = second

    for sweep in range(SWEEPS):
        for pair in range(4):
            if sweep == 0:
                for b in (2 * pair, 2 * pair + 1):
                    for copy in loads[b]:
                        copy.wait()
            for block in range(blocks):
                carry(pair, pl.ds(block * LANES, LANES))
        for number, target in enumerate((even, odd)):
            rows = pl.ds(256 * number, 256)
            first = smoothing[number, :, pl.ds(0, 256)]
            second = smoothing[number, :, pl.ds(256, 256)]
            target[...] = (
                dot32(first, high[rows, :]) + dot32(second, high[rows, :]) + dot32(first, low[rows, :])
            )
        for b in range(8):
            bottom, top, bottom_moved, top_moved = [], [], [], []
            for block in range(blocks):
                lanes = pl.ds(block * LANES, LANES)
                e = even[pl.ds(8 * b, 8), lanes]
                o = odd[pl.ds(8 * b, 8), lanes]
                bottom.append(e + o)
                top.append(e - o)
                bottom_moved.append(pltpu.roll(bottom[-1], LANES - 1, 1))
                top_moved.append(pltpu.roll(top[-1], 1, 1))
            for block in range(blocks):
                lanes = pl.ds(block * LANES, LANES)
                before = jnp.where(lane == 0, top_moved[block - 1], top_moved[block])
                after = jnp.where(
                    lane == LANES - 1, bottom_moved[(block + 1) % blocks], bottom_moved[block]
                )
                if block == 0:
                    before = jnp.where((lane == 0) & is_first, bottom[0], before)
                if block == blocks - 2:
                    after = jnp.where((lane == LANES - 1) & is_last, top[block], after)
                tx[0, b, :, lanes] = adv[0, b, :, lanes] + (bottom[block] + before)
                tx[7, b, :, lanes] = adv[7, b, :, lanes] + (top[block] + after)
                for k in range(1, 4):
                    e = even[pl.ds(64 * k + 8 * b, 8), lanes]
                    o = odd[pl.ds(64 * k + 8 * b, 8), lanes]
                    tx[k, b, :, lanes] = adv[k, b, :, lanes] + (e + o)
                    tx[7 - k, b, :, lanes] = adv[7 - k, b, :, lanes] + (e - o)

    stores = [
        pltpu.make_async_copy(tx.at[:, b, :, pl.ds(0, count)], t_out.at[:, b], out_sems.at[b])
        for b in range(8)
    ]
    for copy in stores:
        copy.start()
    for block in range(blocks - 1):
        lanes = pl.ds(block * LANES, LANES)
        for side in range(2):
            wall = tx[:, 7 * side, :, lanes].reshape(64, LANES)
            wall_out[pl.ds(64 * side, 64), lanes] = wall
            layer = film[pl.ds(64 * side, 64), lanes]
            faces[side, lanes, :] = jnp.concatenate([layer, layer * wall], axis=0).T

    def scatter(i, _):
        for j in range(128):
            spot = position[i, j]
            sending[pl.ds(spot, 1), :] = faces[j % 2, pl.ds(i * 64 + j // 2, 1), :]
        return 0

    lax.fori_loop(0, 16, scatter, 0)
    for copy in stores:
        copy.wait()


def owner_kernel(arrived, cell, plate, conductivity, plate_op, sheet, returning, hot, parts):
    name = lax.broadcasted_iota(jnp.int32, (512, LANES), 0)
    for i in range(32):
        hot[:, pl.ds(i * LANES, LANES)] = (
            (name == cell[i : i + 1, :]).astype(jnp.float32).astype(jnp.bfloat16)
        )
    for half in range(2):
        for i in range(16):
            block = arrived[pl.ds(8 * i, 8), pl.ds(16 * half, 16), :].reshape(128, LANES)
            first, second = halves(block)
            rows = pl.ds((16 * half + i) * 128, 128)
            parts[rows, pl.ds(0, LANES)] = first
            parts[rows, pl.ds(LANES, LANES)] = second
    both = dot32(hot[...], parts[...])
    total = (both[:, :LANES] + both[:, LANES:]).T
    film_sum = total[:64]
    heat_sum = total[64:]
    contact = (plate[0:64, :] + CONTACT * heat_sum) / (1.0 + CONTACT * film_sum)
    relaxed = jnp.concatenate([contact, plate[64:128, :]], axis=0)
    first, second = halves(relaxed)
    op_first = plate_op[:, pl.ds(0, 128)]
    op_second = plate_op[:, pl.ds(128, 128)]
    spread = dot32(op_first, first) + dot32(op_second, first) + dot32(op_first, second)
    conducted = relaxed + DT_PLATE * conductivity[...] * spread
    sheet[...] = conducted
    first, second = halves(conducted[:64])
    both = dot32(jnp.concatenate([first, second], axis=0), hot[...])
    seen = both[:64] + both[64:]
    for i in range(16):
        block = jnp.concatenate(
            [seen[:, i * 128 : (i + 1) * 128], seen[:, 2048 + i * 128 : 2048 + (i + 1) * 128]], axis=0
        )
        returning[pl.ds(i * 128, 128), :] = block.T


def finish_kernel(returned, position, film, wall, t_in, t_out, contact_out, rows, gathered, out, sems):
    del t_in
    lane = lax.broadcasted_iota(jnp.int32, (16, LANES), 1)
    for q in range(128):
        block = returned[pl.ds(16 * q, 16), :]
        turned = pltpu.roll(block, 64, 1)
        rows[pl.ds(32 * q, 16), :] = jnp.where(lane < 64, block, turned)
        rows[pl.ds(32 * q + 16, 16), :] = jnp.where(lane < 64, turned, block)
    one = lax.broadcasted_iota(jnp.int32, (1, LANES), 1)

    def gather(i, _):
        for j in range(64):
            low = rows[pl.ds(position[i, 2 * j], 1), :]
            high = rows[pl.ds(position[i, 2 * j + 1], 1), :]
            gathered[pl.ds(i * 64 + j, 1), :] = jnp.where(one < 64, low, high)
        return 0

    lax.fori_loop(0, 16, gather, 0)
    for block in range(8):
        lanes = pl.ds(block * LANES, LANES)
        contact = gathered[lanes, :].T
        contact_out[:, lanes] = contact
        own = wall[:, lanes]
        out[:, lanes] = own + MIXING_WEIGHT * (film[:, lanes] * (contact - own))
    copies = []
    for side in range(2):
        for a in range(8):
            copies.append(
                pltpu.make_async_copy(
                    out.at[pl.ds(64 * side + 8 * a, 8)], t_out.at[a, 7 * side], sems.at[side, a]
                )
            )
    for copy in copies:
        copy.start()
    for copy in copies:
        copy.wait()


def vmem():
    return pl.BlockSpec(memory_space=pltpu.VMEM)


def smem():
    return pl.BlockSpec(memory_space=pltpu.SMEM)


def anywhere():
    return pl.BlockSpec(memory_space=pl.ANY)


def params():
    return pltpu.CompilerParams(vmem_limit_bytes=VMEM_LIMIT)


def shards(warmth, velocity, wall_film, face_owner, plate_temp, conductivity, plate_cell):
    from_even, from_odd, smoothing, plate_op = gll_tables()
    f32 = jnp.float32
    count = warmth.shape[1]
    axes = ("flow", "grp")
    devices = lax.axis_size(axes)
    me = lax.axis_index(axes)
    last = count // LANES - 1
    side = jax.ShapeDtypeStruct((8, 512), f32)
    to_next, to_prev = pl.pallas_call(
        edge_kernel,
        grid=(1,),
        out_shape=(side, side),
        in_specs=[
            pl.BlockSpec((512, LANES), lambda i: (0, 0)),
            pl.BlockSpec((512, LANES), lambda i: (0, last)),
            pl.BlockSpec((512, LANES), lambda i: (0, 0)),
            pl.BlockSpec((512, LANES), lambda i: (0, last)),
        ],
        out_specs=[pl.BlockSpec((8, 512), lambda i: (0, 0))] * 2,
        compiler_params=params(),
        name="edges",
    )(warmth, warmth, velocity, velocity)
    up = [(i, i + 1) for i in range(devices - 1)]
    down = [(j, i) for i, j in up]
    from_prev = lax.ppermute(to_next, axes, up)
    from_next = lax.ppermute(to_prev, axes, down)
    position = pl.pallas_call(
        rank_kernel,
        out_shape=jax.ShapeDtypeStruct((16, 128), jnp.int32),
        in_specs=[vmem()],
        out_specs=vmem(),
        compiler_params=params(),
        name="ranks",
    )(face_owner.reshape(16, 128))
    ends = jnp.stack([me == 0, me == devices - 1]).astype(jnp.int32)
    wide = count + LANES
    t_new, wall, sending = pl.pallas_call(
        functools.partial(sweep_kernel, from_even, from_odd),
        out_shape=(
            jax.ShapeDtypeStruct((8, 8, 8, count), f32),
            jax.ShapeDtypeStruct((128, count), f32),
            jax.ShapeDtypeStruct((4096, LANES), f32),
        ),
        in_specs=[smem(), anywhere(), anywhere(), vmem(), vmem(), vmem(), vmem(), smem()],
        out_specs=(anywhere(), vmem(), vmem()),
        scratch_shapes=[
            pltpu.VMEM((8, 8, 8, wide), f32),
            pltpu.VMEM((8, 8, 8, wide), f32),
            pltpu.VMEM((8, 8, 8, wide), f32),
            pltpu.VMEM((512, wide), jnp.bfloat16),
            pltpu.VMEM((512, wide), jnp.bfloat16),
            pltpu.VMEM((256, wide), f32),
            pltpu.VMEM((256, wide), f32),
            pltpu.VMEM((128, 512), f32),
            pltpu.VMEM((2, count, LANES), f32),
            pltpu.SemaphoreType.DMA((2, 8)),
            pltpu.SemaphoreType.DMA((8,)),
        ],
        compiler_params=params(),
        name="sweeps",
    )(
        ends,
        warmth.reshape(8, 8, 8, count),
        velocity.reshape(8, 8, 8, count),
        wall_film,
        from_prev,
        from_next,
        jnp.asarray(smoothing),
        position,
    )
    arrived = lax.all_to_all(
        sending.reshape(128, 32, LANES), axes, split_axis=0, concat_axis=0, tiled=True
    )
    cell = plate_cell.reshape(128, 2, 16).transpose(1, 0, 2).reshape(32, LANES)
    sheet, returning = pl.pallas_call(
        owner_kernel,
        out_shape=(
            jax.ShapeDtypeStruct((128, 512), f32),
            jax.ShapeDtypeStruct((2048, LANES), f32),
        ),
        in_specs=[vmem()] * 5,
        out_specs=(vmem(), vmem()),
        scratch_shapes=[
            pltpu.VMEM((512, 4096), jnp.bfloat16),
            pltpu.VMEM((4096, 256), jnp.bfloat16),
        ],
        compiler_params=params(),
        name="plates",
    )(arrived, cell, plate_temp, conductivity, jnp.asarray(plate_op))
    returned = lax.all_to_all(
        returning.reshape(128, 16, LANES), axes, split_axis=0, concat_axis=0, tiled=True
    )
    coolant, boundary = pl.pallas_call(
        finish_kernel,
        out_shape=(
            jax.ShapeDtypeStruct((8, 8, 8, count), f32),
            jax.ShapeDtypeStruct((128, count), f32),
        ),
        in_specs=[vmem(), smem(), vmem(), vmem(), anywhere()],
        out_specs=(anywhere(), vmem()),
        scratch_shapes=[
            pltpu.VMEM((4096, LANES), f32),
            pltpu.VMEM((count, LANES), f32),
            pltpu.VMEM((128, count), f32),
            pltpu.SemaphoreType.DMA((2, 8)),
        ],
        input_output_aliases={4: 0},
        compiler_params=params(),
        name="finish",
    )(returned.reshape(2048, LANES), position, wall_film, wall, t_new)
    return coolant.reshape(512, count), boundary, sheet


def solution(mesh):
    placed = (
        P(None, ("flow", "grp")),
        P(None, ("flow", "grp")),
        P(None, ("flow", "grp")),
        P(("flow", "grp"), None),
        P(None, ("flow", "grp")),
        P(None, ("flow", "grp")),
        P(("flow", "grp")),
    )
    return jax.shard_map(
        shards,
        mesh=mesh,
        in_specs=placed,
        out_specs=(P(None, ("flow", "grp")), P(None, ("flow", "grp")), P(None, ("flow", "grp"))),
        check_vma=False,
    )
```

```python
import functools

import jax
import jax.numpy as jnp
import ml_dtypes
import numpy as np
from jax import lax
from jax.experimental import pallas as pl
from jax.experimental.pallas import tpu as pltpu
from jax.sharding import PartitionSpec as P

SWEEPS = 2
LAMBDA_H = 4.0
DAMPING_RATIO = 0.5
CARRY_STEP_SIZE = 0.05
CONTACT = 0.1
DT_PLATE = 0.0008
COUPLE = 20.0
MIXING_WEIGHT = 0.5
GLL_POINTS = (
    -1.0,
    -0.8717401485096066,
    -0.5917001814331423,
    -0.2092992179024789,
    0.2092992179024789,
    0.5917001814331423,
    0.8717401485096066,
    1.0,
)
GLL_WEIGHTS = (
    0.03571428571428571,
    0.2107042271435061,
    0.3411226924835044,
    0.4124587946587038,
    0.4124587946587038,
    0.3411226924835044,
    0.2107042271435061,
    0.03571428571428571,
)
LANES = 128


def split_pair(table):
    high = np.asarray(table, np.float32).astype(ml_dtypes.bfloat16)
    low = (np.asarray(table, np.float64) - high.astype(np.float64)).astype(np.float32)
    return high, low.astype(ml_dtypes.bfloat16)


def gll_tables():
    points = np.array(GLL_POINTS)
    weights = np.array(GLL_WEIGHTS)
    identity = np.eye(8)
    spread = points[:, None] - points[None, :] + identity
    bary_weight = 1.0 / np.prod(spread, axis=1)
    gradient = bary_weight[None, :] / bary_weight[:, None] / spread
    gradient = gradient * (1.0 - identity)
    gradient = gradient - identity * gradient.sum(axis=1)[:, None]
    stiffness = gradient.T * weights[None, :] @ gradient
    strong = stiffness / weights[:, None]
    ratio = np.diag(strong)
    laplace = (
        np.kron(np.kron(strong, identity), identity)
        + np.kron(np.kron(identity, strong), identity)
        + np.kron(np.kron(identity, identity), strong)
    )
    diagonal = (
        LAMBDA_H + ratio[:, None, None] + ratio[None, :, None] + ratio[None, None, :]
    ).reshape(512)
    share = np.ones((8, 64))
    share[0] = 0.5
    share[7] = 0.5
    smooth = -DAMPING_RATIO * (share.reshape(512) / diagonal)[:, None] * laplace
    quad = smooth.reshape(8, 64, 8, 64)
    near = quad[:4, :, :4, :]
    far = quad[:4, :, 7:3:-1, :]
    even = (0.5 * (near + far)).reshape(256, 256)
    odd = (0.5 * (near - far)).reshape(256, 256)
    carry = -CARRY_STEP_SIZE * gradient
    from_even = 0.5 * (carry[:4, :4] + carry[:4, 7:3:-1])
    from_odd = 0.5 * (carry[:4, :4] - carry[:4, 7:3:-1])
    weight_matrix = np.diag(weights)
    in_plane = (np.kron(stiffness, weight_matrix) + np.kron(weight_matrix, stiffness)) / np.kron(
        weights, weights
    )[:, None]
    through = np.array([[-1.0, 1.0], [1.0, -1.0]])
    plate_op = -np.kron(np.eye(2), in_plane) + COUPLE * np.kron(through, np.eye(64))
    even_parts = split_pair(even)
    odd_parts = split_pair(odd)
    smoothing = np.stack(
        [np.concatenate(even_parts, 1), np.concatenate(odd_parts, 1)]
    )
    plate_parts = np.concatenate(split_pair(plate_op), 1)
    return from_even, from_odd, smoothing, plate_parts


def halves(value):
    high = value.astype(jnp.bfloat16)
    low = (value - high.astype(jnp.float32)).astype(jnp.bfloat16)
    return high, low


def dot32(a, b):
    return jnp.dot(a, b, preferred_element_type=jnp.float32)


def edge_kernel(t_in, v_in, to_next, to_prev, held, sems):
    count = t_in.shape[1]
    copies = []
    for i, array in enumerate((t_in, v_in)):
        for j, start in enumerate((0, count - LANES)):
            copy = pltpu.make_async_copy(
                array.at[:, pl.ds(start, LANES)], held.at[i, j], sems.at[i, j]
            )
            copy.start()
            copies.append(copy)
    for copy in copies:
        copy.wait()
    for i in range(2):
        to_prev[pl.ds(2 * i, 2), :] = held[i, 0].T[0:2, :]
        to_next[pl.ds(2 * i, 2), :] = held[i, 1].T[126:128, :]
    to_prev[4:8, :] = jnp.ones((4, 512), jnp.float32)
    to_next[4:8, :] = jnp.ones((4, 512), jnp.float32)


def fill_positions(owner, position):
    wide = 256
    row = lax.broadcasted_iota(jnp.int32, (wide, wide), 0)
    col = lax.broadcasted_iota(jnp.int32, (wide, wide), 1)
    upto = (row <= col).astype(jnp.float32).astype(jnp.bfloat16)
    name = lax.broadcasted_iota(jnp.int32, (128, LANES), 0)
    before = jnp.zeros((128, 1), jnp.float32)
    for step in range(8):
        pair = [
            (name == owner[2 * step + i : 2 * step + i + 1, :]).astype(jnp.float32)
            for i in range(2)
        ]
        hot = jnp.concatenate(pair, axis=1)
        seen = dot32(hot.astype(jnp.bfloat16), upto)
        rank = jnp.sum(hot * (seen + before), axis=0, keepdims=True) - 1.0
        before = before + seen[:, wide - 1 : wide]
        for i in range(2):
            at = slice(2 * step + i, 2 * step + i + 1)
            position[at, :] = owner[at, :] * 32 + rank[:, i * LANES : (i + 1) * LANES].astype(
                jnp.int32
            )


def carry(from_even, from_odd, t, v, adv, high, low, pair, block):
    at = pl.ds(2 * pair, 2)
    lanes = pl.ds(block * LANES, LANES)
    e = [t[k] + t[7 - k] for k in range(4)]
    o = [t[k] - t[7 - k] for k in range(4)]
    for i in range(4):
        p = sum(float(from_even[i, j]) * e[j] for j in range(4))
        q = sum(float(from_odd[i, j]) * o[j] for j in range(4))
        near = t[i] + v[i] * (q + p)
        far = t[7 - i] + v[7 - i] * (q - p)
        adv[i, at, :, lanes] = near.reshape(2, 8, LANES)
        adv[7 - i, at, :, lanes] = far.reshape(2, 8, LANES)
        for number, part in enumerate((near + far, near - far)):
            first, second = halves(part)
            rows = pl.ds(256 * number + 64 * i + 16 * pair, 16)
            high[rows, lanes] = first
            low[rows, lanes] = second


def smooth(smoothing, high, low, even, odd, group):
    lanes = pl.ds(group[0] * LANES, len(group) * LANES)
    for number, target in enumerate((even, odd)):
        rows = pl.ds(256 * number, 256)
        first = smoothing[number, :, pl.ds(0, 256)]
        second = smoothing[number, :, pl.ds(256, 256)]
        target[:, lanes] = (
            dot32(first, high[rows, lanes])
            + dot32(second, high[rows, lanes])
            + dot32(first, low[rows, lanes])
        )


def slab(array, a, pair, block):
    return array[a, pl.ds(2 * pair, 2), :, pl.ds(block * LANES, LANES)].reshape(16, LANES)


def begin_kernel(
    from_even,
    from_odd,
    t_in,
    v_in,
    film_in,
    smoothing_in,
    owner,
    v,
    adv,
    even,
    odd,
    film,
    smoothing,
    position,
    t,
    high,
    low,
    sems,
):
    count = t_in.shape[-1]
    groups = [[2 * i, 2 * i + 1] for i in range(count // LANES // 2)]
    loads = []
    for number, group in enumerate(groups):
        lanes = pl.ds(group[0] * LANES, 2 * LANES)
        loads.append(
            (
                pltpu.make_async_copy(t_in.at[:, :, :, lanes], t.at[:, :, :, lanes], sems.at[0, number]),
                pltpu.make_async_copy(v_in.at[:, :, :, lanes], v.at[:, :, :, lanes], sems.at[1, number]),
            )
        )
    smoothing_copy = pltpu.make_async_copy(smoothing_in, smoothing, sems.at[0, 4])
    film_copy = pltpu.make_async_copy(film_in, film, sems.at[1, 4])
    for copy in loads[0] + (smoothing_copy,) + sum(loads[1:], ()) + (film_copy,):
        copy.start()
    fill_positions(owner, position)
    for number, group in enumerate(groups):
        for copy in loads[number]:
            copy.wait()
        for pair in range(4):
            for block in group:
                carry(
                    from_even,
                    from_odd,
                    [slab(t, a, pair, block) for a in range(8)],
                    [slab(v, a, pair, block) for a in range(8)],
                    adv,
                    high,
                    low,
                    pair,
                    block,
                )
        if number == 0:
            smoothing_copy.wait()
        smooth(smoothing, high, low, even, odd, group)
    film_copy.wait()


def sweep_kernel(
    from_even,
    from_odd,
    v,
    adv,
    even_first,
    odd_first,
    film,
    smoothing,
    from_prev,
    from_next,
    position_in,
    t_out,
    wall_out,
    sending,
    position,
    wall,
    t_edge,
    v_edge,
    adv_edge,
    high_edge,
    low_edge,
    even_edge,
    odd_edge,
    t_new,
    adv_second,
    high,
    low,
    even_second,
    odd_second,
    edge,
    faces,
    in_sem,
    out_sems,
):
    position_copy = pltpu.make_async_copy(position_in, position, in_sem)
    position_copy.start()
    count = v.shape[-1]
    inner = count // LANES
    blocks = inner + 1
    groups = [[2 * i, 2 * i + 1] for i in range(inner // 2)]
    edge[...] = jnp.zeros_like(edge)
    for i, array in enumerate((t_edge, v_edge)):
        edge[0:2, :] = from_next[pl.ds(2 * i, 2), :]
        edge[126:128, :] = from_prev[pl.ds(2 * i, 2), :]
        array[...] = edge[...].T.reshape(8, 8, 8, LANES)
    sending[...] = jnp.zeros_like(sending)
    lane = lax.broadcasted_iota(jnp.int32, (16, LANES), 1)
    is_first = (lane == 0) & (from_prev[4:5, 0:LANES] == 0.0)
    is_last = (lane == LANES - 1) & (from_next[4:5, 0:LANES] == 0.0)

    def part(even, odd, k, pair, block):
        at = (pl.ds(64 * k + 16 * pair, 16), pl.ds((block % inner) * LANES, LANES))
        if block == inner:
            return even_edge[at], odd_edge[at]
        return even[at], odd[at]

    def combine(even, odd, start, pair, block):
        own = [part(even, odd, k, pair, block) for k in range(4)]
        bottom = own[0][0] + own[0][1]
        top = own[0][0] - own[0][1]
        e, o = part(even, odd, 0, pair, (block - 1) % blocks)
        before = pltpu.roll(jnp.where(lane == LANES - 1, e - o, top), 1, 1)
        e, o = part(even, odd, 0, pair, (block + 1) % blocks)
        after = pltpu.roll(jnp.where(lane == 0, e + o, bottom), LANES - 1, 1)
        if block == 0:
            before = jnp.where(is_first, bottom, before)
        if block == inner - 1:
            after = jnp.where(is_last, top, after)
        change = [None] * 8
        change[0] = bottom + before
        change[7] = top + after
        for k in range(1, 4):
            change[k] = own[k][0] + own[k][1]
            change[7 - k] = own[k][0] - own[k][1]
        return [slab(start, a, pair, block % inner) + change[a] for a in range(8)]

    def carry_edge(t, pair):
        carry(
            from_even,
            from_odd,
            t,
            [slab(v_edge, a, pair, 0) for a in range(8)],
            adv_edge,
            high_edge,
            low_edge,
            pair,
            0,
        )

    for pair in range(4):
        carry_edge([slab(t_edge, a, pair, 0) for a in range(8)], pair)
    smooth(smoothing, high_edge, low_edge, even_edge, odd_edge, [0])
    for group in groups:
        for pair in range(4):
            for block in group:
                carry(
                    from_even,
                    from_odd,
                    combine(even_first, odd_first, adv, pair, block),
                    [slab(v, a, pair, block) for a in range(8)],
                    adv_second,
                    high,
                    low,
                    pair,
                    block,
                )
        smooth(smoothing, high, low, even_second, odd_second, group)
    for pair in range(4):
        carry_edge(combine(even_first, odd_first, adv_edge, pair, inner), pair)
    smooth(smoothing, high_edge, low_edge, even_edge, odd_edge, [0])
    stores = []
    for number, group in enumerate(groups):
        for block in group:
            lanes = pl.ds(block * LANES, LANES)
            for pair in range(4):
                t = combine(even_second, odd_second, adv_second, pair, block)
                for a in range(8):
                    t_new[a, pl.ds(2 * pair, 2), :, lanes] = t[a].reshape(2, 8, LANES)
            for side in range(2):
                own = t_new[:, 7 * side, :, lanes].reshape(64, LANES)
                wall[pl.ds(64 * side, 64), lanes] = own
                layer = film[pl.ds(64 * side, 64), lanes]
                faces[side, lanes, :] = jnp.concatenate([layer, layer * own], axis=0).T
        lanes = pl.ds(group[0] * LANES, 2 * LANES)
        copy = pltpu.make_async_copy(
            t_new.at[:, :, :, lanes], t_out.at[:, :, :, lanes], out_sems.at[number]
        )
        copy.start()
        stores.append(copy)
    copy = pltpu.make_async_copy(wall, wall_out, out_sems.at[4])
    copy.start()
    stores.append(copy)
    position_copy.wait()

    def scatter(i, _):
        for j in range(128):
            spot = position[i, j]
            sending[pl.ds(spot, 1), :] = faces[j % 2, pl.ds(i * 64 + j // 2, 1), :]
        return 0

    lax.fori_loop(0, 16, scatter, 0)
    for copy in stores:
        copy.wait()


def owner_kernel(
    arrived,
    cell,
    plate_in,
    conductivity_in,
    plate_op_in,
    sheet_out,
    returning,
    hot,
    parts,
    plate,
    conductivity,
    plate_op,
    sheet,
    in_sems,
    out_sem,
):
    loads = [
        pltpu.make_async_copy(plate_in, plate, in_sems.at[0]),
        pltpu.make_async_copy(conductivity_in, conductivity, in_sems.at[1]),
        pltpu.make_async_copy(plate_op_in, plate_op, in_sems.at[2]),
    ]
    for copy in loads:
        copy.start()
    name = lax.broadcasted_iota(jnp.int32, (512, LANES), 0)
    both = 0.0
    for chunk in range(4):
        for i in range(8):
            place = 8 * chunk + i
            block = arrived[
                pl.ds(8 * (place % 16), 8), pl.ds(16 * (place // 16), 16), :
            ].reshape(128, LANES)
            first, second = halves(block)
            rows = pl.ds(place * 128, 128)
            parts[rows, pl.ds(0, LANES)] = first
            parts[rows, pl.ds(LANES, LANES)] = second
            hot[:, rows] = (
                (name == cell[place : place + 1, :]).astype(jnp.float32).astype(jnp.bfloat16)
            )
        slots = pl.ds(1024 * chunk, 1024)
        both = both + dot32(hot[:, slots], parts[slots, :])
    total = (both[:, :LANES] + both[:, LANES:]).T
    film_sum = total[:64]
    heat_sum = total[64:]
    for copy in loads:
        copy.wait()
    contact = (plate[0:64, :] + CONTACT * heat_sum) / (1.0 + CONTACT * film_sum)
    relaxed = jnp.concatenate([contact, plate[64:128, :]], axis=0)
    first, second = halves(relaxed)
    op_first = plate_op[:, pl.ds(0, 128)]
    op_second = plate_op[:, pl.ds(128, 128)]
    spread = dot32(op_first, first) + dot32(op_second, first) + dot32(op_first, second)
    conducted = relaxed + DT_PLATE * conductivity[...] * spread
    sheet[...] = conducted
    store = pltpu.make_async_copy(sheet, sheet_out, out_sem)
    store.start()
    first, second = halves(conducted[:64])
    mixed = jnp.concatenate([first, second], axis=0)
    for i in range(16):
        low = dot32(mixed, hot[:, pl.ds(i * 128, 128)])
        high = dot32(mixed, hot[:, pl.ds(2048 + i * 128, 128)])
        block = jnp.concatenate([low[:64] + low[64:], high[:64] + high[64:]], axis=0)
        returning[pl.ds(i * 128, 128), :] = block.T
    store.wait()


def finish_kernel(
    returned,
    position_in,
    film_in,
    wall_in,
    t_in,
    t_out,
    contact_out,
    position,
    film,
    wall,
    rows,
    gathered,
    contact,
    out,
    in_sems,
    out_sems,
):
    del t_in
    loads = [
        pltpu.make_async_copy(position_in, position, in_sems.at[0]),
        pltpu.make_async_copy(film_in, film, in_sems.at[1]),
        pltpu.make_async_copy(wall_in, wall, in_sems.at[2]),
    ]
    for copy in loads:
        copy.start()
    lane = lax.broadcasted_iota(jnp.int32, (16, LANES), 1)

    def expand(i, _):
        for k in range(8):
            block = returned[pl.ds(128 * i + 16 * k, 16), :]
            turned = pltpu.roll(block, 64, 1)
            at = 256 * i + 32 * k
            rows[pl.ds(at, 16), :] = jnp.where(lane < 64, block, turned)
            rows[pl.ds(at + 16, 16), :] = jnp.where(lane < 64, turned, block)
        return 0

    lax.fori_loop(0, 16, expand, 0)
    loads[0].wait()
    one = lax.broadcasted_iota(jnp.int32, (1, LANES), 1)
    stores = []
    for block in range(8):

        def gather(i, _):
            for j in range(64):
                low = rows[pl.ds(position[2 * block + i, 2 * j], 1), :]
                high = rows[pl.ds(position[2 * block + i, 2 * j + 1], 1), :]
                gathered[pl.ds(i * 64 + j, 1), :] = jnp.where(one < 64, low, high)
            return 0

        lax.fori_loop(0, 2, gather, 0)
        if block == 0:
            loads[1].wait()
            loads[2].wait()
        lanes = pl.ds(block * LANES, LANES)
        seen = gathered[...].T
        contact[:, lanes] = seen
        own = wall[:, lanes]
        out[:, :, :, lanes] = (
            own + MIXING_WEIGHT * (film[:, lanes] * (seen - own))
        ).reshape(2, 8, 8, LANES)
        copies = [
            pltpu.make_async_copy(
                contact.at[:, lanes], contact_out.at[:, lanes], out_sems.at[block, 0]
            )
        ] + [
            pltpu.make_async_copy(
                out.at[side, :, :, lanes], t_out.at[:, 7 * side, :, lanes], out_sems.at[block, 1 + side]
            )
            for side in range(2)
        ]
        for copy in copies:
            copy.start()
        stores += copies
    for copy in stores:
        copy.wait()


def vmem():
    return pl.BlockSpec(memory_space=pltpu.VMEM)


def smem():
    return pl.BlockSpec(memory_space=pltpu.SMEM)


def hbm():
    return pl.BlockSpec(memory_space=pltpu.HBM)


def far(array):
    return pltpu.with_memory_space_constraint(array, pltpu.HBM)


def params(mebibytes):
    return pltpu.CompilerParams(vmem_limit_bytes=mebibytes * 1024 * 1024)


def edges(warmth, velocity):
    side = jax.ShapeDtypeStruct((8, 512), jnp.float32)
    return pl.pallas_call(
        edge_kernel,
        out_shape=(side, side),
        in_specs=[hbm(), hbm()],
        out_specs=(vmem(), vmem()),
        scratch_shapes=[
            pltpu.VMEM((2, 2, 512, LANES), jnp.float32),
            pltpu.SemaphoreType.DMA((2, 2)),
        ],
        compiler_params=params(4),
        name="edges",
    )(far(warmth), far(velocity))


def begin(warmth, velocity, wall_film, owner):
    f32 = jnp.float32
    from_even, from_odd, smoothing, _ = gll_tables()
    count = warmth.shape[1]
    return pl.pallas_call(
        functools.partial(begin_kernel, from_even, from_odd),
        out_shape=(
            pltpu.VMEM((8, 8, 8, count), f32),
            pltpu.VMEM((8, 8, 8, count), f32),
            pltpu.VMEM((256, count), f32),
            pltpu.VMEM((256, count), f32),
            pltpu.VMEM((128, count), f32),
            pltpu.VMEM((2, 256, 512), jnp.bfloat16),
            jax.ShapeDtypeStruct((16, 128), jnp.int32),
        ),
        in_specs=[hbm(), hbm(), hbm(), hbm(), vmem()],
        out_specs=(vmem(),) * 7,
        scratch_shapes=[
            pltpu.VMEM((8, 8, 8, count), f32),
            pltpu.VMEM((512, count), jnp.bfloat16),
            pltpu.VMEM((512, count), jnp.bfloat16),
            pltpu.SemaphoreType.DMA((2, 5)),
        ],
        compiler_params=params(20),
        name="begin",
    )(
        far(warmth.reshape(8, 8, 8, count)),
        far(velocity.reshape(8, 8, 8, count)),
        far(wall_film),
        far(jnp.asarray(smoothing)),
        owner,
    )


def sweeps(v, adv, even, odd, film, smoothing, from_prev, from_next, position):
    f32 = jnp.float32
    bf16 = jnp.bfloat16
    from_even, from_odd, _, _ = gll_tables()
    count = v.shape[-1]
    near = [pltpu.with_memory_space_constraint(x, pltpu.VMEM) for x in (v, adv, even, odd, film, smoothing)]
    return pl.pallas_call(
        functools.partial(sweep_kernel, from_even, from_odd),
        out_shape=(
            jax.ShapeDtypeStruct((8, 8, 8, count), f32),
            pltpu.HBM((128, count), f32),
            jax.ShapeDtypeStruct((4096, LANES), f32),
        ),
        in_specs=[vmem()] * 8 + [hbm()],
        out_specs=(hbm(), hbm(), vmem()),
        scratch_shapes=[
            pltpu.SMEM((16, 128), jnp.int32),
            pltpu.VMEM((128, count), f32),
            pltpu.VMEM((8, 8, 8, LANES), f32),
            pltpu.VMEM((8, 8, 8, LANES), f32),
            pltpu.VMEM((8, 8, 8, LANES), f32),
            pltpu.VMEM((512, LANES), bf16),
            pltpu.VMEM((512, LANES), bf16),
            pltpu.VMEM((256, LANES), f32),
            pltpu.VMEM((256, LANES), f32),
            pltpu.VMEM((8, 8, 8, count), f32),
            pltpu.VMEM((8, 8, 8, count), f32),
            pltpu.VMEM((512, count), bf16),
            pltpu.VMEM((512, count), bf16),
            pltpu.VMEM((256, count), f32),
            pltpu.VMEM((256, count), f32),
            pltpu.VMEM((128, 512), f32),
            pltpu.VMEM((2, count, LANES), f32),
            pltpu.SemaphoreType.DMA(()),
            pltpu.SemaphoreType.DMA((5,)),
        ],
        compiler_params=params(28),
        name="sweeps",
    )(*near, from_prev, from_next, position)


def plates(arrived, cell, plate_temp, conductivity):
    f32 = jnp.float32
    plate_op = gll_tables()[3]
    return pl.pallas_call(
        owner_kernel,
        out_shape=(
            jax.ShapeDtypeStruct((128, 512), f32),
            jax.ShapeDtypeStruct((2048, LANES), f32),
        ),
        in_specs=[vmem(), vmem(), hbm(), hbm(), hbm()],
        out_specs=(hbm(), vmem()),
        scratch_shapes=[
            pltpu.VMEM((512, 4096), jnp.bfloat16),
            pltpu.VMEM((4096, 256), jnp.bfloat16),
            pltpu.VMEM((128, 512), f32),
            pltpu.VMEM((128, 512), f32),
            pltpu.VMEM((128, 256), jnp.bfloat16),
            pltpu.VMEM((128, 512), f32),
            pltpu.SemaphoreType.DMA((3,)),
            pltpu.SemaphoreType.DMA(()),
        ],
        compiler_params=params(20),
        name="plates",
    )(arrived, cell, far(plate_temp), far(conductivity), far(jnp.asarray(plate_op)))


def finish(returned, position, wall_film, wall, t_new):
    f32 = jnp.float32
    count = wall.shape[1]
    return pl.pallas_call(
        finish_kernel,
        out_shape=(
            jax.ShapeDtypeStruct((8, 8, 8, count), f32),
            jax.ShapeDtypeStruct((128, count), f32),
        ),
        in_specs=[vmem(), hbm(), hbm(), hbm(), hbm()],
        out_specs=(hbm(), hbm()),
        scratch_shapes=[
            pltpu.SMEM((16, 128), jnp.int32),
            pltpu.VMEM((128, count), f32),
            pltpu.VMEM((128, count), f32),
            pltpu.VMEM((4096, LANES), f32),
            pltpu.VMEM((LANES, LANES), f32),
            pltpu.VMEM((128, count), f32),
            pltpu.VMEM((2, 8, 8, count), f32),
            pltpu.SemaphoreType.DMA((3,)),
            pltpu.SemaphoreType.DMA((8, 3)),
        ],
        input_output_aliases={4: 0},
        compiler_params=params(12),
        name="finish",
    )(returned, far(position), far(wall_film), far(wall), t_new)


def shards(warmth, velocity, wall_film, face_owner, plate_temp, conductivity, plate_cell):
    count = warmth.shape[1]
    axes = ("flow", "grp")
    devices = lax.axis_size(axes)

    def exchange(rows):
        return lax.all_to_all(rows, axes, split_axis=0, concat_axis=0, tiled=True)

    to_next, to_prev = edges(warmth, velocity)
    up = [(i, i + 1) for i in range(devices - 1)]
    down = [(j, i) for i, j in up]
    from_prev = lax.ppermute(to_next, axes, up)
    from_next = lax.ppermute(to_prev, axes, down)
    *started, position = begin(warmth, velocity, wall_film, face_owner.reshape(16, 128))
    t_new, wall, sending = sweeps(*started, from_prev, from_next, position)
    cell = plate_cell.reshape(128, 2, 16).transpose(1, 0, 2).reshape(32, LANES)
    cell, sending = lax.optimization_barrier((cell, sending))
    arrived = exchange(sending.reshape(128, 32, LANES))
    sheet, returning = plates(arrived, cell, plate_temp, conductivity)
    returned = exchange(returning.reshape(128, 16, LANES)).reshape(2048, LANES)
    coolant, boundary = finish(returned, position, wall_film, wall, t_new)
    return coolant.reshape(512, count), boundary, sheet


def solution(mesh):
    placed = (
        P(None, ("flow", "grp")),
        P(None, ("flow", "grp")),
        P(None, ("flow", "grp")),
        P(("flow", "grp"), None),
        P(None, ("flow", "grp")),
        P(None, ("flow", "grp")),
        P(("flow", "grp")),
    )
    return jax.shard_map(
        shards,
        mesh=mesh,
        in_specs=placed,
        out_specs=(P(None, ("flow", "grp")), P(None, ("flow", "grp")), P(None, ("flow", "grp"))),
        check_vma=False,
    )
```

```python
import functools

import jax
import jax.numpy as jnp
import ml_dtypes
import numpy as np
from jax import lax
from jax.experimental import pallas as pl
from jax.experimental.pallas import tpu as pltpu
from jax.sharding import PartitionSpec as P

SWEEPS = 2
LAMBDA_H = 4.0
DAMPING_RATIO = 0.5
CARRY_STEP_SIZE = 0.05
CONTACT = 0.1
DT_PLATE = 0.0008
COUPLE = 20.0
MIXING_WEIGHT = 0.5
GLL_POINTS = (
    -1.0,
    -0.8717401485096066,
    -0.5917001814331423,
    -0.2092992179024789,
    0.2092992179024789,
    0.5917001814331423,
    0.8717401485096066,
    1.0,
)
GLL_WEIGHTS = (
    0.03571428571428571,
    0.2107042271435061,
    0.3411226924835044,
    0.4124587946587038,
    0.4124587946587038,
    0.3411226924835044,
    0.2107042271435061,
    0.03571428571428571,
)
LANES = 128


def split_pair(table):
    high = np.asarray(table, np.float32).astype(ml_dtypes.bfloat16)
    low = (np.asarray(table, np.float64) - high.astype(np.float64)).astype(np.float32)
    return high, low.astype(ml_dtypes.bfloat16)


def gll_tables():
    points = np.array(GLL_POINTS)
    weights = np.array(GLL_WEIGHTS)
    identity = np.eye(8)
    spread = points[:, None] - points[None, :] + identity
    bary_weight = 1.0 / np.prod(spread, axis=1)
    gradient = bary_weight[None, :] / bary_weight[:, None] / spread
    gradient = gradient * (1.0 - identity)
    gradient = gradient - identity * gradient.sum(axis=1)[:, None]
    stiffness = gradient.T * weights[None, :] @ gradient
    strong = stiffness / weights[:, None]
    ratio = np.diag(strong)
    laplace = (
        np.kron(np.kron(strong, identity), identity)
        + np.kron(np.kron(identity, strong), identity)
        + np.kron(np.kron(identity, identity), strong)
    )
    diagonal = (
        LAMBDA_H + ratio[:, None, None] + ratio[None, :, None] + ratio[None, None, :]
    ).reshape(512)
    share = np.ones((8, 64))
    share[0] = 0.5
    share[7] = 0.5
    smooth = -DAMPING_RATIO * (share.reshape(512) / diagonal)[:, None] * laplace
    quad = smooth.reshape(8, 64, 8, 64)
    near = quad[:4, :, :4, :]
    far = quad[:4, :, 7:3:-1, :]
    even = (0.5 * (near + far)).reshape(256, 256)
    odd = (0.5 * (near - far)).reshape(256, 256)
    carry = -CARRY_STEP_SIZE * gradient
    from_even = 0.5 * (carry[:4, :4] + carry[:4, 7:3:-1])
    from_odd = 0.5 * (carry[:4, :4] - carry[:4, 7:3:-1])
    weight_matrix = np.diag(weights)
    in_plane = (np.kron(stiffness, weight_matrix) + np.kron(weight_matrix, stiffness)) / np.kron(
        weights, weights
    )[:, None]
    through = np.array([[-1.0, 1.0], [1.0, -1.0]])
    plate_op = -np.kron(np.eye(2), in_plane) + COUPLE * np.kron(through, np.eye(64))
    even_parts = split_pair(even)
    odd_parts = split_pair(odd)
    smoothing = np.stack(
        [np.concatenate(even_parts, 1), np.concatenate(odd_parts, 1)]
    )
    plate_parts = np.concatenate(split_pair(plate_op), 1)
    return from_even, from_odd, smoothing, plate_parts


def halves(value):
    high = value.astype(jnp.bfloat16)
    low = (value - high.astype(jnp.float32)).astype(jnp.bfloat16)
    return high, low


def dot32(a, b):
    return jnp.dot(a, b, preferred_element_type=jnp.float32)


def edge_kernel(t_in, v_in, to_next, to_prev, held, sems):
    count = t_in.shape[1]
    copies = []
    for i, array in enumerate((t_in, v_in)):
        for j, start in enumerate((0, count - LANES)):
            copy = pltpu.make_async_copy(
                array.at[:, pl.ds(start, LANES)], held.at[i, j], sems.at[i, j]
            )
            copy.start()
            copies.append(copy)
    for copy in copies:
        copy.wait()
    for i in range(2):
        to_prev[pl.ds(2 * i, 2), :] = held[i, 0].T[0:2, :]
        to_next[pl.ds(2 * i, 2), :] = held[i, 1].T[126:128, :]
    to_prev[4:8, :] = jnp.ones((4, 512), jnp.float32)
    to_next[4:8, :] = jnp.ones((4, 512), jnp.float32)


def fill_positions(owner, position):
    wide = 256
    row = lax.broadcasted_iota(jnp.int32, (wide, wide), 0)
    col = lax.broadcasted_iota(jnp.int32, (wide, wide), 1)
    upto = (row <= col).astype(jnp.float32).astype(jnp.bfloat16)
    name = lax.broadcasted_iota(jnp.int32, (128, LANES), 0)
    before = jnp.zeros((128, 1), jnp.float32)
    for step in range(8):
        pair = [
            (name == owner[2 * step + i : 2 * step + i + 1, :]).astype(jnp.float32)
            for i in range(2)
        ]
        hot = jnp.concatenate(pair, axis=1)
        seen = dot32(hot.astype(jnp.bfloat16), upto)
        rank = jnp.sum(hot * (seen + before), axis=0, keepdims=True) - 1.0
        before = before + seen[:, wide - 1 : wide]
        for i in range(2):
            at = slice(2 * step + i, 2 * step + i + 1)
            position[at, :] = owner[at, :] * 32 + rank[:, i * LANES : (i + 1) * LANES].astype(
                jnp.int32
            )


def carry(from_even, from_odd, start, v, adv, high, low, pair, block):
    lanes = pl.ds(block * LANES, LANES)
    parts = []
    for b in (2 * pair, 2 * pair + 1):
        t = start(b)
        e = [t[k] + t[7 - k] for k in range(4)]
        o = [t[k] - t[7 - k] for k in range(4)]
        kept = []
        for i in range(4):
            p = float(from_even[i, 0]) * e[0]
            q = float(from_odd[i, 0]) * o[0]
            for j in range(1, 4):
                p = p + float(from_even[i, j]) * e[j]
                q = q + float(from_odd[i, j]) * o[j]
            near = t[i] + v[i, b, :, lanes] * (q + p)
            far = t[7 - i] + v[7 - i, b, :, lanes] * (q - p)
            adv[i, b, :, lanes] = near
            adv[7 - i, b, :, lanes] = far
            kept.append((near + far, near - far))
        parts.append(kept)
    for i in range(4):
        for number in range(2):
            first, second = halves(
                jnp.concatenate([parts[0][i][number], parts[1][i][number]], axis=0)
            )
            rows = pl.ds(256 * number + 64 * i + 16 * pair, 16)
            high[rows, lanes] = first
            low[rows, lanes] = second


def smooth(smoothing, high, low, even, odd, group):
    lanes = pl.ds(group[0] * LANES, len(group) * LANES)
    for number, target in enumerate((even, odd)):
        rows = pl.ds(256 * number, 256)
        first = smoothing[number, :, pl.ds(0, 256)]
        second = smoothing[number, :, pl.ds(256, 256)]
        target[:, lanes] = (
            dot32(first, high[rows, lanes])
            + dot32(second, high[rows, lanes])
            + dot32(first, low[rows, lanes])
        )


def begin_kernel(
    from_even,
    from_odd,
    t_in,
    v_in,
    film_in,
    smoothing_in,
    owner,
    v,
    adv,
    even,
    odd,
    film,
    smoothing,
    position,
    t,
    high,
    low,
    sems,
):
    count = t_in.shape[-1]
    groups = [[2 * i, 2 * i + 1] for i in range(count // LANES // 2)]
    loads = []
    for number, group in enumerate(groups):
        lanes = pl.ds(group[0] * LANES, 2 * LANES)
        loads.append(
            (
                pltpu.make_async_copy(t_in.at[:, :, :, lanes], t.at[:, :, :, lanes], sems.at[0, number]),
                pltpu.make_async_copy(v_in.at[:, :, :, lanes], v.at[:, :, :, lanes], sems.at[1, number]),
            )
        )
    smoothing_copy = pltpu.make_async_copy(smoothing_in, smoothing, sems.at[0, 4])
    film_copy = pltpu.make_async_copy(film_in, film, sems.at[1, 4])
    for copy in loads[0] + (smoothing_copy,) + sum(loads[1:], ()) + (film_copy,):
        copy.start()
    fill_positions(owner, position)
    for number, group in enumerate(groups):
        for copy in loads[number]:
            copy.wait()
        for pair in range(4):
            for block in group:
                lanes = pl.ds(block * LANES, LANES)
                carry(
                    from_even,
                    from_odd,
                    lambda b: [t[a, b, :, lanes] for a in range(8)],
                    v,
                    adv,
                    high,
                    low,
                    pair,
                    block,
                )
        if number > 0:
            smooth(smoothing, high, low, even, odd, groups[number - 1])
        else:
            smoothing_copy.wait()
    smooth(smoothing, high, low, even, odd, groups[-1])
    film_copy.wait()


def sweep_kernel(
    from_even,
    from_odd,
    v,
    adv,
    even_first,
    odd_first,
    film,
    smoothing,
    from_prev,
    from_next,
    position_in,
    t_out,
    wall_out,
    sending,
    position,
    wall,
    t_edge,
    v_edge,
    adv_edge,
    high_edge,
    low_edge,
    even_edge,
    odd_edge,
    t_new,
    adv_second,
    high,
    low,
    even_second,
    odd_second,
    edge,
    faces,
    in_sem,
    out_sems,
):
    position_copy = pltpu.make_async_copy(position_in, position, in_sem)
    position_copy.start()
    count = v.shape[-1]
    inner = count // LANES
    blocks = inner + 1
    groups = [[2 * i, 2 * i + 1] for i in range(inner // 2)]
    edge[...] = jnp.zeros_like(edge)
    for i, array in enumerate((t_edge, v_edge)):
        edge[0:2, :] = from_next[pl.ds(2 * i, 2), :]
        edge[126:128, :] = from_prev[pl.ds(2 * i, 2), :]
        array[...] = edge[...].T.reshape(8, 8, 8, LANES)
    sending[...] = jnp.zeros_like(sending)
    lane = lax.broadcasted_iota(jnp.int32, (8, LANES), 1)
    is_first = (lane == 0) & (from_prev[4:5, 0:LANES] == 0.0)
    is_last = (lane == LANES - 1) & (from_next[4:5, 0:LANES] == 0.0)

    changes = ((even_first, odd_first), (even_second, odd_second))

    def part(sweep, k, b, block):
        rows = pl.ds(64 * k + 8 * b, 8)
        if block == inner:
            return even_edge[sweep, rows, :], odd_edge[sweep, rows, :]
        even, odd = changes[sweep]
        lanes = pl.ds(block * LANES, LANES)
        return even[rows, lanes], odd[rows, lanes]

    def combine(sweep, start, b, block):
        e, o = part(sweep, 0, b, block)
        bottom, top = e + o, e - o
        e, o = part(sweep, 0, b, (block - 1) % blocks)
        before = pltpu.roll(jnp.where(lane == LANES - 1, e - o, top), 1, 1)
        e, o = part(sweep, 0, b, (block + 1) % blocks)
        after = pltpu.roll(jnp.where(lane == 0, e + o, bottom), LANES - 1, 1)
        if block == 0:
            before = jnp.where(is_first, bottom, before)
        if block == inner - 1:
            after = jnp.where(is_last, top, after)
        lanes = pl.ds((block % inner) * LANES, LANES)
        t = [None] * 8
        t[0] = start[0, b, :, lanes] + (bottom + before)
        t[7] = start[7, b, :, lanes] + (top + after)
        for k in range(1, 4):
            e, o = part(sweep, k, b, block)
            t[k] = start[k, b, :, lanes] + (e + o)
            t[7 - k] = start[7 - k, b, :, lanes] + (e - o)
        return t

    def carry_edge(sweep, start):
        into = adv_edge.at[sweep]
        for pair in range(4):
            carry(from_even, from_odd, start, v_edge, into, high_edge, low_edge, pair, 0)
        smooth(
            smoothing, high_edge, low_edge, even_edge.at[sweep], odd_edge.at[sweep], [0]
        )

    def carry_inner(group):
        for pair in range(4):
            for block in group:
                carry(
                    from_even,
                    from_odd,
                    functools.partial(combine, 0, adv, block=block),
                    v,
                    adv_second,
                    high,
                    low,
                    pair,
                    block,
                )

    stores = []

    def complete(number):
        group = groups[number]
        for block in group:
            lanes = pl.ds(block * LANES, LANES)
            for b in range(8):
                t = combine(1, adv_second, b, block)
                for a in range(8):
                    t_new[a, b, :, lanes] = t[a]
            for side in range(2):
                own = t_new[:, 7 * side, :, lanes].reshape(64, LANES)
                wall[pl.ds(64 * side, 64), lanes] = own
                layer = film[pl.ds(64 * side, 64), lanes]
                faces[side, lanes, :] = jnp.concatenate([layer, layer * own], axis=0).T
            for j in range(2 * LANES):
                spot = position[2 * block + j // LANES, j % LANES]
                sending[pl.ds(spot, 1), :] = faces[j % 2, pl.ds(block * LANES + j // 2, 1), :]
        lanes = pl.ds(group[0] * LANES, 2 * LANES)
        copy = pltpu.make_async_copy(
            t_new.at[:, :, :, lanes], t_out.at[:, :, :, lanes], out_sems.at[number]
        )
        copy.start()
        stores.append(copy)

    carry_edge(0, lambda b: [t_edge[a, b, :, :] for a in range(8)])
    carry_inner(groups[0])
    carry_edge(1, functools.partial(combine, 0, adv_edge.at[0], block=inner))
    position_copy.wait()
    smooth(smoothing, high, low, even_second, odd_second, groups[0])
    for number in range(1, len(groups)):
        carry_inner(groups[number])
        smooth(smoothing, high, low, even_second, odd_second, groups[number])
        complete(number - 1)
    complete(len(groups) - 1)
    copy = pltpu.make_async_copy(wall, wall_out, out_sems.at[4])
    copy.start()
    stores.append(copy)
    for copy in stores:
        copy.wait()


def owner_kernel(
    arrived,
    cell,
    plate_in,
    conductivity_in,
    plate_op_in,
    sheet_out,
    returning,
    hot,
    parts,
    plate,
    conductivity,
    plate_op,
    sheet,
    in_sems,
    out_sem,
):
    loads = [
        pltpu.make_async_copy(plate_in, plate, in_sems.at[0]),
        pltpu.make_async_copy(conductivity_in, conductivity, in_sems.at[1]),
        pltpu.make_async_copy(plate_op_in, plate_op, in_sems.at[2]),
    ]
    for copy in loads:
        copy.start()
    name = lax.broadcasted_iota(jnp.int32, (512, LANES), 0).astype(jnp.int16)
    one, zero = jnp.bfloat16(1), jnp.bfloat16(0)
    both = [None, None]
    for chunk in range(4):
        for i in range(8):
            place = 8 * chunk + i
            block = arrived[
                pl.ds(8 * (place % 16), 8), pl.ds(16 * (place // 16), 16), :
            ].reshape(128, LANES)
            first, second = halves(block)
            rows = pl.ds(place * 128, 128)
            parts[rows, pl.ds(0, LANES)] = first
            parts[rows, pl.ds(LANES, LANES)] = second
            hot[:, rows] = jnp.where(
                name == cell[place : place + 1, :].astype(jnp.int16), one, zero
            )
        slots = pl.ds(1024 * chunk, 1024)
        for i in range(2):
            share = dot32(hot[pl.ds(256 * i, 256), slots], parts[slots, :])
            both[i] = share if chunk == 0 else both[i] + share
    both = jnp.concatenate(both, axis=0)
    total = (both[:, :LANES] + both[:, LANES:]).T
    film_sum = total[:64]
    heat_sum = total[64:]
    for copy in loads:
        copy.wait()
    contact = (plate[0:64, :] + CONTACT * heat_sum) / (1.0 + CONTACT * film_sum)
    relaxed = jnp.concatenate([contact, plate[64:128, :]], axis=0)
    first, second = halves(relaxed)
    op_first = plate_op[:, pl.ds(0, 128)]
    op_second = plate_op[:, pl.ds(128, 128)]
    spread = dot32(op_first, first) + dot32(op_second, first) + dot32(op_first, second)
    conducted = relaxed + DT_PLATE * conductivity[...] * spread
    sheet[...] = conducted
    store = pltpu.make_async_copy(sheet, sheet_out, out_sem)
    store.start()
    first, second = halves(conducted[:64])
    mixed = jnp.concatenate([first, second], axis=0)
    seen = dot32(mixed, hot[...])
    seen = seen[:64] + seen[64:]
    for i in range(16):
        block = jnp.concatenate(
            [seen[:, i * 128 : (i + 1) * 128], seen[:, 2048 + i * 128 : 2048 + (i + 1) * 128]], axis=0
        )
        returning[pl.ds(i * 128, 128), :] = block.T
    store.wait()


def finish_kernel(
    returned,
    position_in,
    film_in,
    wall_in,
    t_in,
    t_out,
    contact_out,
    position,
    film,
    wall,
    rows,
    gathered,
    contact,
    out,
    in_sems,
    out_sems,
):
    del t_in
    loads = [
        pltpu.make_async_copy(position_in, position, in_sems.at[0]),
        pltpu.make_async_copy(film_in, film, in_sems.at[1]),
        pltpu.make_async_copy(wall_in, wall, in_sems.at[2]),
    ]
    for copy in loads:
        copy.start()
    lane = lax.broadcasted_iota(jnp.int32, (16, LANES), 1)

    def expand(i, _):
        for k in range(8):
            block = returned[pl.ds(128 * i + 16 * k, 16), :]
            turned = pltpu.roll(block, 64, 1)
            at = 256 * i + 32 * k
            rows[pl.ds(at, 16), :] = jnp.where(lane < 64, block, turned)
            rows[pl.ds(at + 16, 16), :] = jnp.where(lane < 64, turned, block)
        return 0

    lax.fori_loop(0, 16, expand, 0)
    loads[0].wait()
    one = lax.broadcasted_iota(jnp.int32, (1, LANES), 1)
    stores = []
    for block in range(8):
        for j in range(LANES):
            i, k = 2 * block + j // 64, 2 * (j % 64)
            low = rows[pl.ds(position[i, k], 1), :]
            high = rows[pl.ds(position[i, k + 1], 1), :]
            gathered[pl.ds(j, 1), :] = jnp.where(one < 64, low, high)
        if block == 0:
            loads[1].wait()
            loads[2].wait()
        lanes = pl.ds(block * LANES, LANES)
        seen = gathered[...].T
        contact[:, lanes] = seen
        own = wall[:, lanes]
        out[:, :, :, lanes] = (
            own + MIXING_WEIGHT * (film[:, lanes] * (seen - own))
        ).reshape(2, 8, 8, LANES)
        copies = [
            pltpu.make_async_copy(
                contact.at[:, lanes], contact_out.at[:, lanes], out_sems.at[block, 0]
            )
        ] + [
            pltpu.make_async_copy(
                out.at[side, :, :, lanes], t_out.at[:, 7 * side, :, lanes], out_sems.at[block, 1 + side]
            )
            for side in range(2)
        ]
        for copy in copies:
            copy.start()
        stores += copies
    for copy in stores:
        copy.wait()


def vmem():
    return pl.BlockSpec(memory_space=pltpu.VMEM)


def smem():
    return pl.BlockSpec(memory_space=pltpu.SMEM)


def hbm():
    return pl.BlockSpec(memory_space=pltpu.HBM)


def far(array):
    return pltpu.with_memory_space_constraint(array, pltpu.HBM)


def params(mebibytes):
    return pltpu.CompilerParams(vmem_limit_bytes=mebibytes * 1024 * 1024)


def edges(warmth, velocity):
    side = jax.ShapeDtypeStruct((8, 512), jnp.float32)
    return pl.pallas_call(
        edge_kernel,
        out_shape=(side, side),
        in_specs=[hbm(), hbm()],
        out_specs=(vmem(), vmem()),
        scratch_shapes=[
            pltpu.VMEM((2, 2, 512, LANES), jnp.float32),
            pltpu.SemaphoreType.DMA((2, 2)),
        ],
        compiler_params=params(4),
        name="edges",
    )(far(warmth), far(velocity))


def begin(warmth, velocity, wall_film, owner):
    f32 = jnp.float32
    from_even, from_odd, smoothing, _ = gll_tables()
    count = warmth.shape[1]
    return pl.pallas_call(
        functools.partial(begin_kernel, from_even, from_odd),
        out_shape=(
            pltpu.VMEM((8, 8, 8, count), f32),
            pltpu.VMEM((8, 8, 8, count), f32),
            pltpu.VMEM((256, count), f32),
            pltpu.VMEM((256, count), f32),
            pltpu.VMEM((128, count), f32),
            pltpu.VMEM((2, 256, 512), jnp.bfloat16),
            jax.ShapeDtypeStruct((16, 128), jnp.int32),
        ),
        in_specs=[hbm(), hbm(), hbm(), hbm(), vmem()],
        out_specs=(vmem(),) * 7,
        scratch_shapes=[
            pltpu.VMEM((8, 8, 8, count), f32),
            pltpu.VMEM((512, count), jnp.bfloat16),
            pltpu.VMEM((512, count), jnp.bfloat16),
            pltpu.SemaphoreType.DMA((2, 5)),
        ],
        compiler_params=params(20),
        name="begin",
    )(
        far(warmth.reshape(8, 8, 8, count)),
        far(velocity.reshape(8, 8, 8, count)),
        far(wall_film),
        far(jnp.asarray(smoothing)),
        owner,
    )


def sweeps(v, adv, even, odd, film, smoothing, from_prev, from_next, position):
    f32 = jnp.float32
    bf16 = jnp.bfloat16
    from_even, from_odd, _, _ = gll_tables()
    count = v.shape[-1]
    near = [pltpu.with_memory_space_constraint(x, pltpu.VMEM) for x in (v, adv, even, odd, film, smoothing)]
    return pl.pallas_call(
        functools.partial(sweep_kernel, from_even, from_odd),
        out_shape=(
            jax.ShapeDtypeStruct((8, 8, 8, count), f32),
            pltpu.HBM((128, count), f32),
            jax.ShapeDtypeStruct((4096, LANES), f32),
        ),
        in_specs=[vmem()] * 8 + [hbm()],
        out_specs=(hbm(), hbm(), vmem()),
        scratch_shapes=[
            pltpu.SMEM((16, 128), jnp.int32),
            pltpu.VMEM((128, count), f32),
            pltpu.VMEM((8, 8, 8, LANES), f32),
            pltpu.VMEM((8, 8, 8, LANES), f32),
            pltpu.VMEM((2, 8, 8, 8, LANES), f32),
            pltpu.VMEM((512, LANES), bf16),
            pltpu.VMEM((512, LANES), bf16),
            pltpu.VMEM((2, 256, LANES), f32),
            pltpu.VMEM((2, 256, LANES), f32),
            pltpu.VMEM((8, 8, 8, count), f32),
            pltpu.VMEM((8, 8, 8, count), f32),
            pltpu.VMEM((512, count), bf16),
            pltpu.VMEM((512, count), bf16),
            pltpu.VMEM((256, count), f32),
            pltpu.VMEM((256, count), f32),
            pltpu.VMEM((128, 512), f32),
            pltpu.VMEM((2, count, LANES), f32),
            pltpu.SemaphoreType.DMA(()),
            pltpu.SemaphoreType.DMA((5,)),
        ],
        compiler_params=params(28),
        name="sweeps",
    )(*near, from_prev, from_next, position)


def plates(arrived, cell, plate_temp, conductivity):
    f32 = jnp.float32
    plate_op = gll_tables()[3]
    return pl.pallas_call(
        owner_kernel,
        out_shape=(
            jax.ShapeDtypeStruct((128, 512), f32),
            jax.ShapeDtypeStruct((2048, LANES), f32),
        ),
        in_specs=[vmem(), vmem(), hbm(), hbm(), hbm()],
        out_specs=(hbm(), vmem()),
        scratch_shapes=[
            pltpu.VMEM((512, 4096), jnp.bfloat16),
            pltpu.VMEM((4096, 256), jnp.bfloat16),
            pltpu.VMEM((128, 512), f32),
            pltpu.VMEM((128, 512), f32),
            pltpu.VMEM((128, 256), jnp.bfloat16),
            pltpu.VMEM((128, 512), f32),
            pltpu.SemaphoreType.DMA((3,)),
            pltpu.SemaphoreType.DMA(()),
        ],
        compiler_params=params(20),
        name="plates",
    )(arrived, cell, far(plate_temp), far(conductivity), far(jnp.asarray(plate_op)))


def finish(returned, position, wall_film, wall, t_new):
    f32 = jnp.float32
    count = wall.shape[1]
    return pl.pallas_call(
        finish_kernel,
        out_shape=(
            jax.ShapeDtypeStruct((8, 8, 8, count), f32),
            jax.ShapeDtypeStruct((128, count), f32),
        ),
        in_specs=[vmem(), hbm(), hbm(), hbm(), hbm()],
        out_specs=(hbm(), hbm()),
        scratch_shapes=[
            pltpu.SMEM((16, 128), jnp.int32),
            pltpu.VMEM((128, count), f32),
            pltpu.VMEM((128, count), f32),
            pltpu.VMEM((4096, LANES), f32),
            pltpu.VMEM((LANES, LANES), f32),
            pltpu.VMEM((128, count), f32),
            pltpu.VMEM((2, 8, 8, count), f32),
            pltpu.SemaphoreType.DMA((3,)),
            pltpu.SemaphoreType.DMA((8, 3)),
        ],
        input_output_aliases={4: 0},
        compiler_params=params(12),
        name="finish",
    )(returned, far(position), far(wall_film), far(wall), t_new)


def shards(warmth, velocity, wall_film, face_owner, plate_temp, conductivity, plate_cell):
    count = warmth.shape[1]
    axes = ("flow", "grp")
    devices = lax.axis_size(axes)

    def exchange(rows):
        return lax.all_to_all(rows, axes, split_axis=0, concat_axis=0, tiled=True)

    to_next, to_prev = edges(warmth, velocity)
    up = [(i, i + 1) for i in range(devices - 1)]
    down = [(j, i) for i, j in up]
    from_prev = lax.ppermute(to_next, axes, up)
    from_next = lax.ppermute(to_prev, axes, down)
    *started, position = begin(warmth, velocity, wall_film, face_owner.reshape(16, 128))
    t_new, wall, sending = sweeps(*started, from_prev, from_next, position)
    cell = plate_cell.reshape(128, 2, 16).transpose(1, 0, 2).reshape(32, LANES)
    cell, sending = lax.optimization_barrier((cell, sending))
    arrived = exchange(sending.reshape(128, 32, LANES))
    sheet, returning = plates(arrived, cell, plate_temp, conductivity)
    returned = exchange(returning.reshape(128, 16, LANES)).reshape(2048, LANES)
    coolant, boundary = finish(returned, position, wall_film, wall, t_new)
    return coolant.reshape(512, count), boundary, sheet


def solution(mesh):
    placed = (
        P(None, ("flow", "grp")),
        P(None, ("flow", "grp")),
        P(None, ("flow", "grp")),
        P(("flow", "grp"), None),
        P(None, ("flow", "grp")),
        P(None, ("flow", "grp")),
        P(("flow", "grp")),
    )
    return jax.shard_map(
        shards,
        mesh=mesh,
        in_specs=placed,
        out_specs=(P(None, ("flow", "grp")), P(None, ("flow", "grp")), P(None, ("flow", "grp"))),
        check_vma=False,
    )
```

```python
import functools

import jax
import jax.numpy as jnp
import ml_dtypes
import numpy as np
from jax import lax
from jax.experimental import pallas as pl
from jax.experimental.pallas import tpu as pltpu
from jax.sharding import PartitionSpec as P

SWEEPS = 2
LAMBDA_H = 4.0
DAMPING_RATIO = 0.5
CARRY_STEP_SIZE = 0.05
CONTACT = 0.1
DT_PLATE = 0.0008
COUPLE = 20.0
MIXING_WEIGHT = 0.5
GLL_POINTS = (
    -1.0,
    -0.8717401485096066,
    -0.5917001814331423,
    -0.2092992179024789,
    0.2092992179024789,
    0.5917001814331423,
    0.8717401485096066,
    1.0,
)
GLL_WEIGHTS = (
    0.03571428571428571,
    0.2107042271435061,
    0.3411226924835044,
    0.4124587946587038,
    0.4124587946587038,
    0.3411226924835044,
    0.2107042271435061,
    0.03571428571428571,
)
LANES = 128


def split_pair(table):
    high = np.asarray(table, np.float32).astype(ml_dtypes.bfloat16)
    low = (np.asarray(table, np.float64) - high.astype(np.float64)).astype(np.float32)
    return high, low.astype(ml_dtypes.bfloat16)


def gll_tables():
    points = np.array(GLL_POINTS)
    weights = np.array(GLL_WEIGHTS)
    identity = np.eye(8)
    spread = points[:, None] - points[None, :] + identity
    bary_weight = 1.0 / np.prod(spread, axis=1)
    gradient = bary_weight[None, :] / bary_weight[:, None] / spread
    gradient = gradient * (1.0 - identity)
    gradient = gradient - identity * gradient.sum(axis=1)[:, None]
    stiffness = gradient.T * weights[None, :] @ gradient
    strong = stiffness / weights[:, None]
    ratio = np.diag(strong)
    laplace = (
        np.kron(np.kron(strong, identity), identity)
        + np.kron(np.kron(identity, strong), identity)
        + np.kron(np.kron(identity, identity), strong)
    )
    diagonal = (
        LAMBDA_H + ratio[:, None, None] + ratio[None, :, None] + ratio[None, None, :]
    ).reshape(512)
    share = np.ones((8, 64))
    share[0] = 0.5
    share[7] = 0.5
    smooth = -DAMPING_RATIO * (share.reshape(512) / diagonal)[:, None] * laplace
    quad = smooth.reshape(8, 64, 8, 64)
    near = quad[:4, :, :4, :]
    far = quad[:4, :, 7:3:-1, :]
    even = (0.5 * (near + far)).reshape(256, 256)
    odd = (0.5 * (near - far)).reshape(256, 256)
    carry = -CARRY_STEP_SIZE * gradient
    from_even = 0.5 * (carry[:4, :4] + carry[:4, 7:3:-1])
    from_odd = 0.5 * (carry[:4, :4] - carry[:4, 7:3:-1])
    weight_matrix = np.diag(weights)
    in_plane = (np.kron(stiffness, weight_matrix) + np.kron(weight_matrix, stiffness)) / np.kron(
        weights, weights
    )[:, None]
    through = np.array([[-1.0, 1.0], [1.0, -1.0]])
    plate_op = -np.kron(np.eye(2), in_plane) + COUPLE * np.kron(through, np.eye(64))
    even_parts = split_pair(even)
    odd_parts = split_pair(odd)
    smoothing = np.stack(
        [np.concatenate(even_parts, 1), np.concatenate(odd_parts, 1)]
    )
    plate_parts = np.concatenate(split_pair(plate_op), 1)
    return from_even, from_odd, smoothing, plate_parts


def halves(value):
    high = value.astype(jnp.bfloat16)
    low = (value - high.astype(jnp.float32)).astype(jnp.bfloat16)
    return high, low


def dot32(a, b):
    return jnp.dot(a, b, preferred_element_type=jnp.float32)


def edge_kernel(t_in, v_in, to_first, to_second, held, sems):
    count = t_in.shape[1]
    copies = []
    for i, array in enumerate((t_in, v_in)):
        for j, start in enumerate((0, count - LANES)):
            copy = pltpu.make_async_copy(
                array.at[:, pl.ds(start, LANES)], held.at[i, j], sems.at[i, j]
            )
            copy.start()
            copies.append(copy)
    for copy in copies:
        copy.wait()
    odd = lax.axis_index("grp") % 2 == 1
    for i in range(2):
        rows = pl.ds(2 * i, 2)
        bottom = held[i, 0].T[0:2, :]
        top = held[i, 1].T[126:128, :]
        to_first[rows, :] = jnp.where(odd, bottom, top)
        to_second[rows, :] = jnp.where(odd, top, bottom)
    to_first[4:8, :] = jnp.ones((4, 512), jnp.float32)
    to_second[4:8, :] = jnp.ones((4, 512), jnp.float32)


def fill_positions(owner, position):
    wide = 256
    row = lax.broadcasted_iota(jnp.int32, (wide, wide), 0)
    col = lax.broadcasted_iota(jnp.int32, (wide, wide), 1)
    upto = (row <= col).astype(jnp.float32).astype(jnp.bfloat16)
    name = lax.broadcasted_iota(jnp.int32, (128, LANES), 0)
    before = jnp.zeros((128, 1), jnp.float32)
    for step in range(8):
        pair = [
            (name == owner[2 * step + i : 2 * step + i + 1, :]).astype(jnp.float32)
            for i in range(2)
        ]
        hot = jnp.concatenate(pair, axis=1)
        seen = dot32(hot.astype(jnp.bfloat16), upto)
        rank = jnp.sum(hot * (seen + before), axis=0, keepdims=True) - 1.0
        before = before + seen[:, wide - 1 : wide]
        for i in range(2):
            at = slice(2 * step + i, 2 * step + i + 1)
            position[at, :] = owner[at, :] * 32 + rank[:, i * LANES : (i + 1) * LANES].astype(
                jnp.int32
            )


def carry(from_even, from_odd, start, v, adv, high, low, pair, block):
    lanes = pl.ds(block * LANES, LANES)
    parts = []
    for b in (2 * pair, 2 * pair + 1):
        t = start(b)
        e = [t[k] + t[7 - k] for k in range(4)]
        o = [t[k] - t[7 - k] for k in range(4)]
        kept = []
        for i in range(4):
            p = float(from_even[i, 0]) * e[0]
            q = float(from_odd[i, 0]) * o[0]
            for j in range(1, 4):
                p = p + float(from_even[i, j]) * e[j]
                q = q + float(from_odd[i, j]) * o[j]
            near = t[i] + v[i, b, :, lanes] * (q + p)
            far = t[7 - i] + v[7 - i, b, :, lanes] * (q - p)
            adv[i, b, :, lanes] = near
            adv[7 - i, b, :, lanes] = far
            kept.append((near + far, near - far))
        parts.append(kept)
    for i in range(4):
        for number in range(2):
            first, second = halves(
                jnp.concatenate([parts[0][i][number], parts[1][i][number]], axis=0)
            )
            rows = pl.ds(256 * number + 64 * i + 16 * pair, 16)
            high[rows, lanes] = first
            low[rows, lanes] = second


def smooth(smoothing, high, low, even, odd, group):
    lanes = pl.ds(group[0] * LANES, len(group) * LANES)
    for number, target in enumerate((even, odd)):
        rows = pl.ds(256 * number, 256)
        first = smoothing[number, :, pl.ds(0, 256)]
        second = smoothing[number, :, pl.ds(256, 256)]
        target[:, lanes] = (
            dot32(first, high[rows, lanes])
            + dot32(second, high[rows, lanes])
            + dot32(first, low[rows, lanes])
        )


def begin_kernel(
    from_even,
    from_odd,
    t,
    v_in,
    film_in,
    smoothing_in,
    owner,
    v,
    adv,
    even,
    odd,
    film,
    smoothing,
    position,
    high,
    low,
    sems,
):
    count = t.shape[-1]
    groups = [[2 * i, 2 * i + 1] for i in range(count // LANES // 2)]
    smoothing_copy = pltpu.make_async_copy(smoothing_in, smoothing, sems.at[0])
    film_copy = pltpu.make_async_copy(film_in, film, sems.at[1])
    v_copies = []
    for number, group in enumerate(groups):
        lanes = pl.ds(group[0] * LANES, 2 * LANES)
        v_copies.append(
            pltpu.make_async_copy(
                v_in.at[:, :, :, lanes], v.at[:, :, :, lanes], sems.at[2 + number]
            )
        )
    for copy in [v_copies[0], smoothing_copy] + v_copies[1:] + [film_copy]:
        copy.start()
    fill_positions(owner, position)

    def advect(group):
        for pair in range(4):
            for block in group:
                lanes = pl.ds(block * LANES, LANES)
                carry(
                    from_even,
                    from_odd,
                    lambda b: [t[a, b, :, lanes] for a in range(8)],
                    v,
                    adv,
                    high,
                    low,
                    pair,
                    block,
                )

    v_copies[0].wait()
    advect(groups[0])
    smoothing_copy.wait()
    for copy in v_copies[1:]:
        copy.wait()
    for number in range(1, len(groups)):
        advect(groups[number])
        smooth(smoothing, high, low, even, odd, groups[number - 1])
    smooth(smoothing, high, low, even, odd, groups[-1])
    film_copy.wait()


def sweep_kernel(
    from_even,
    from_odd,
    v,
    adv,
    even_first,
    odd_first,
    film,
    smoothing,
    from_first,
    from_second,
    position_in,
    t_out,
    wall_out,
    sending,
    position,
    wall,
    t_edge,
    v_edge,
    adv_edge,
    high_edge,
    low_edge,
    even_edge,
    odd_edge,
    t_new,
    adv_second,
    high,
    low,
    even_second,
    odd_second,
    edge,
    faces,
    in_sem,
    out_sems,
):
    position_copy = pltpu.make_async_copy(position_in, position, in_sem)
    position_copy.start()
    count = v.shape[-1]
    inner = count // LANES
    blocks = inner + 1
    groups = [[2 * i, 2 * i + 1] for i in range(inner // 2)]
    odd = lax.axis_index("grp") % 2 == 1
    from_prev = jnp.where(odd, from_first[...], from_second[...])
    from_next = jnp.where(odd, from_second[...], from_first[...])
    edge[...] = jnp.zeros_like(edge)
    for i, array in enumerate((t_edge, v_edge)):
        edge[0:2, :] = from_next[2 * i : 2 * i + 2, :]
        edge[126:128, :] = from_prev[2 * i : 2 * i + 2, :]
        array[...] = edge[...].T.reshape(8, 8, 8, LANES)
    sending[...] = jnp.zeros_like(sending)
    lane = lax.broadcasted_iota(jnp.int32, (8, LANES), 1)
    is_first = (lane == 0) & (from_prev[4:5, 0:LANES] == 0.0)
    is_last = (lane == LANES - 1) & (from_next[4:5, 0:LANES] == 0.0)

    changes = ((even_first, odd_first), (even_second, odd_second))

    def part(sweep, k, b, block):
        rows = pl.ds(64 * k + 8 * b, 8)
        if block == inner:
            return even_edge[sweep, rows, :], odd_edge[sweep, rows, :]
        even, odd = changes[sweep]
        lanes = pl.ds(block * LANES, LANES)
        return even[rows, lanes], odd[rows, lanes]

    def combine(sweep, start, b, block):
        e, o = part(sweep, 0, b, block)
        bottom, top = e + o, e - o
        e, o = part(sweep, 0, b, (block - 1) % blocks)
        before = pltpu.roll(jnp.where(lane == LANES - 1, e - o, top), 1, 1)
        e, o = part(sweep, 0, b, (block + 1) % blocks)
        after = pltpu.roll(jnp.where(lane == 0, e + o, bottom), LANES - 1, 1)
        if block == 0:
            before = jnp.where(is_first, bottom, before)
        if block == inner - 1:
            after = jnp.where(is_last, top, after)
        lanes = pl.ds((block % inner) * LANES, LANES)
        t = [None] * 8
        t[0] = start[0, b, :, lanes] + (bottom + before)
        t[7] = start[7, b, :, lanes] + (top + after)
        for k in range(1, 4):
            e, o = part(sweep, k, b, block)
            t[k] = start[k, b, :, lanes] + (e + o)
            t[7 - k] = start[7 - k, b, :, lanes] + (e - o)
        return t

    def carry_edge(sweep, start):
        into = adv_edge.at[sweep]
        for pair in range(4):
            carry(from_even, from_odd, start, v_edge, into, high_edge, low_edge, pair, 0)
        smooth(
            smoothing, high_edge, low_edge, even_edge.at[sweep], odd_edge.at[sweep], [0]
        )

    def carry_inner(group):
        for pair in range(4):
            for block in group:
                carry(
                    from_even,
                    from_odd,
                    functools.partial(combine, 0, adv, block=block),
                    v,
                    adv_second,
                    high,
                    low,
                    pair,
                    block,
                )

    stores = []

    def complete(number):
        group = groups[number]
        for block in group:
            lanes = pl.ds(block * LANES, LANES)
            for b in range(8):
                t = combine(1, adv_second, b, block)
                for a in range(8):
                    t_new[a, b, :, lanes] = t[a]
            for side in range(2):
                own = t_new[:, 7 * side, :, lanes].reshape(64, LANES)
                wall[pl.ds(64 * side, 64), lanes] = own
                layer = film[pl.ds(64 * side, 64), lanes]
                faces[side, lanes, :] = jnp.concatenate([layer, layer * own], axis=0).T
            for j in range(2 * LANES):
                spot = position[2 * block + j // LANES, j % LANES]
                sending[pl.ds(spot, 1), :] = faces[j % 2, pl.ds(block * LANES + j // 2, 1), :]
        lanes = pl.ds(group[0] * LANES, 2 * LANES)
        copy = pltpu.make_async_copy(
            t_new.at[:, :, :, lanes], t_out.at[:, :, :, lanes], out_sems.at[number]
        )
        copy.start()
        stores.append(copy)

    carry_edge(0, lambda b: [t_edge[a, b, :, :] for a in range(8)])
    carry_inner(groups[0])
    carry_edge(1, functools.partial(combine, 0, adv_edge.at[0], block=inner))
    position_copy.wait()
    smooth(smoothing, high, low, even_second, odd_second, groups[0])
    for number in range(1, len(groups)):
        carry_inner(groups[number])
        smooth(smoothing, high, low, even_second, odd_second, groups[number])
        complete(number - 1)
    complete(len(groups) - 1)
    copy = pltpu.make_async_copy(wall, wall_out, out_sems.at[4])
    copy.start()
    stores.append(copy)
    for copy in stores:
        copy.wait()


def owner_kernel(
    arrived,
    cell,
    plate_in,
    conductivity_in,
    plate_op_in,
    sheet_out,
    returning,
    hot,
    parts,
    plate,
    conductivity,
    plate_op,
    sheet,
    in_sems,
    out_sem,
):
    loads = [
        pltpu.make_async_copy(plate_in, plate, in_sems.at[0]),
        pltpu.make_async_copy(conductivity_in, conductivity, in_sems.at[1]),
        pltpu.make_async_copy(plate_op_in, plate_op, in_sems.at[2]),
    ]
    for copy in loads:
        copy.start()
    lane = lax.broadcasted_iota(jnp.int32, (16, LANES), 1)
    cells = []
    for half in range(2):
        ordered = jnp.zeros((16, LANES), jnp.int32)
        for i in range(8):
            own = cell[pl.ds(i // 4, 16, stride=2), :]
            shift = (16 * i - 32 * (i % 4) - 16 * half) % LANES
            moved = pltpu.roll(own, shift, 1) if shift else own
            ordered = jnp.where(lane // 16 == i, moved, ordered)
        cells.append(ordered.astype(jnp.int16))
    name = lax.broadcasted_iota(jnp.int32, (512, LANES), 0).astype(jnp.int16)
    one, zero = jnp.bfloat16(1), jnp.bfloat16(0)
    both = [None, None]
    for chunk in range(4):
        for i in range(8):
            place = 8 * chunk + i
            block = arrived[
                pl.ds(8 * (place % 16), 8), pl.ds(16 * (place // 16), 16), :
            ].reshape(128, LANES)
            first, second = halves(block)
            rows = pl.ds(place * 128, 128)
            parts[rows, pl.ds(0, LANES)] = first
            parts[rows, pl.ds(LANES, LANES)] = second
            hot[:, rows] = jnp.where(
                name == cells[place // 16][place % 16 : place % 16 + 1, :], one, zero
            )
        slots = pl.ds(1024 * chunk, 1024)
        for i in range(2):
            share = dot32(hot[pl.ds(256 * i, 256), slots], parts[slots, :])
            both[i] = share if chunk == 0 else both[i] + share
    both = jnp.concatenate(both, axis=0)
    total = (both[:, :LANES] + both[:, LANES:]).T
    film_sum = total[:64]
    heat_sum = total[64:]
    for copy in loads:
        copy.wait()
    contact = (plate[0:64, :] + CONTACT * heat_sum) / (1.0 + CONTACT * film_sum)
    relaxed = jnp.concatenate([contact, plate[64:128, :]], axis=0)
    first, second = halves(relaxed)
    op_first = plate_op[:, pl.ds(0, 128)]
    op_second = plate_op[:, pl.ds(128, 128)]
    spread = dot32(op_first, first) + dot32(op_second, first) + dot32(op_first, second)
    conducted = relaxed + DT_PLATE * conductivity[...] * spread
    sheet[...] = conducted
    store = pltpu.make_async_copy(sheet, sheet_out, out_sem)
    store.start()
    first, second = halves(conducted[:64])
    mixed = jnp.concatenate([first, second], axis=0)
    seen = dot32(mixed, hot[...])
    seen = seen[:64] + seen[64:]
    for i in range(16):
        block = jnp.concatenate(
            [seen[:, i * 128 : (i + 1) * 128], seen[:, 2048 + i * 128 : 2048 + (i + 1) * 128]], axis=0
        )
        returning[pl.ds(i * 128, 128), :] = block.T
    store.wait()


def finish_kernel(
    returned,
    position_in,
    film_in,
    wall_in,
    t_in,
    t_out,
    contact_out,
    position,
    film,
    wall,
    rows,
    gathered,
    contact,
    out,
    in_sems,
    out_sems,
):
    del t_in
    loads = [
        pltpu.make_async_copy(position_in, position, in_sems.at[0]),
        pltpu.make_async_copy(film_in, film, in_sems.at[1]),
        pltpu.make_async_copy(wall_in, wall, in_sems.at[2]),
    ]
    for copy in loads:
        copy.start()
    lane = lax.broadcasted_iota(jnp.int32, (16, LANES), 1)

    def expand(i, _):
        for k in range(8):
            block = returned[pl.ds(128 * i + 16 * k, 16), :]
            turned = pltpu.roll(block, 64, 1)
            at = 256 * i + 32 * k
            rows[pl.ds(at, 16), :] = jnp.where(lane < 64, block, turned)
            rows[pl.ds(at + 16, 16), :] = jnp.where(lane < 64, turned, block)
        return 0

    lax.fori_loop(0, 16, expand, 0)
    loads[0].wait()
    one = lax.broadcasted_iota(jnp.int32, (1, LANES), 1)
    stores = []
    for block in range(8):
        for j in range(LANES):
            i, k = 2 * block + j // 64, 2 * (j % 64)
            low = rows[pl.ds(position[i, k], 1), :]
            high = rows[pl.ds(position[i, k + 1], 1), :]
            gathered[pl.ds(j, 1), :] = jnp.where(one < 64, low, high)
        if block == 0:
            loads[1].wait()
            loads[2].wait()
        lanes = pl.ds(block * LANES, LANES)
        seen = gathered[...].T
        contact[:, lanes] = seen
        own = wall[:, lanes]
        out[:, :, :, lanes] = (
            own + MIXING_WEIGHT * (film[:, lanes] * (seen - own))
        ).reshape(2, 8, 8, LANES)
        copies = [
            pltpu.make_async_copy(
                contact.at[:, lanes], contact_out.at[:, lanes], out_sems.at[block, 0]
            )
        ] + [
            pltpu.make_async_copy(
                out.at[side, :, :, lanes], t_out.at[:, 7 * side, :, lanes], out_sems.at[block, 1 + side]
            )
            for side in range(2)
        ]
        for copy in copies:
            copy.start()
        stores += copies
    for copy in stores:
        copy.wait()


def vmem():
    return pl.BlockSpec(memory_space=pltpu.VMEM)


def smem():
    return pl.BlockSpec(memory_space=pltpu.SMEM)


def hbm():
    return pl.BlockSpec(memory_space=pltpu.HBM)


def far(array):
    return pltpu.with_memory_space_constraint(array, pltpu.HBM)


def params(mebibytes):
    return pltpu.CompilerParams(vmem_limit_bytes=mebibytes * 1024 * 1024)


def edges(warmth, velocity):
    side = jax.ShapeDtypeStruct((8, 512), jnp.float32)
    return pl.pallas_call(
        edge_kernel,
        out_shape=(side, side),
        in_specs=[hbm(), hbm()],
        out_specs=(vmem(), vmem()),
        scratch_shapes=[
            pltpu.VMEM((2, 2, 512, LANES), jnp.float32),
            pltpu.SemaphoreType.DMA((2, 2)),
        ],
        compiler_params=params(4),
        name="edges",
    )(far(warmth), far(velocity))


def near(array):
    return pltpu.with_memory_space_constraint(array, pltpu.VMEM)


def begin(t, v, wall_film, owner):
    f32 = jnp.float32
    from_even, from_odd, smoothing, _ = gll_tables()
    count = t.shape[-1]
    return pl.pallas_call(
        functools.partial(begin_kernel, from_even, from_odd),
        out_shape=(
            pltpu.VMEM((8, 8, 8, count), f32),
            pltpu.VMEM((8, 8, 8, count), f32),
            pltpu.VMEM((256, count), f32),
            pltpu.VMEM((256, count), f32),
            pltpu.VMEM((128, count), f32),
            pltpu.VMEM((2, 256, 512), jnp.bfloat16),
            jax.ShapeDtypeStruct((16, 128), jnp.int32),
        ),
        in_specs=[vmem(), hbm(), hbm(), hbm(), vmem()],
        out_specs=(vmem(),) * 7,
        scratch_shapes=[
            pltpu.VMEM((512, count), jnp.bfloat16),
            pltpu.VMEM((512, count), jnp.bfloat16),
            pltpu.SemaphoreType.DMA((6,)),
        ],
        compiler_params=params(20),
        name="begin",
    )(near(t), far(v), far(wall_film), far(jnp.asarray(smoothing)), owner)


def sweeps(v, adv, even, odd, film, smoothing, from_prev, from_next, position):
    f32 = jnp.float32
    bf16 = jnp.bfloat16
    from_even, from_odd, _, _ = gll_tables()
    count = v.shape[-1]
    held = [near(x) for x in (v, adv, even, odd, film, smoothing)]
    return pl.pallas_call(
        functools.partial(sweep_kernel, from_even, from_odd),
        out_shape=(
            jax.ShapeDtypeStruct((8, 8, 8, count), f32),
            pltpu.HBM((128, count), f32),
            jax.ShapeDtypeStruct((4096, LANES), f32),
        ),
        in_specs=[vmem()] * 8 + [hbm()],
        out_specs=(hbm(), hbm(), vmem()),
        scratch_shapes=[
            pltpu.SMEM((16, 128), jnp.int32),
            pltpu.VMEM((128, count), f32),
            pltpu.VMEM((8, 8, 8, LANES), f32),
            pltpu.VMEM((8, 8, 8, LANES), f32),
            pltpu.VMEM((2, 8, 8, 8, LANES), f32),
            pltpu.VMEM((512, LANES), bf16),
            pltpu.VMEM((512, LANES), bf16),
            pltpu.VMEM((2, 256, LANES), f32),
            pltpu.VMEM((2, 256, LANES), f32),
            pltpu.VMEM((8, 8, 8, count), f32),
            pltpu.VMEM((8, 8, 8, count), f32),
            pltpu.VMEM((512, count), bf16),
            pltpu.VMEM((512, count), bf16),
            pltpu.VMEM((256, count), f32),
            pltpu.VMEM((256, count), f32),
            pltpu.VMEM((128, 512), f32),
            pltpu.VMEM((2, count, LANES), f32),
            pltpu.SemaphoreType.DMA(()),
            pltpu.SemaphoreType.DMA((5,)),
        ],
        compiler_params=params(28),
        name="sweeps",
    )(*held, from_prev, from_next, position)


def plates(arrived, cell, plate_temp, conductivity):
    f32 = jnp.float32
    plate_op = gll_tables()[3]
    return pl.pallas_call(
        owner_kernel,
        out_shape=(
            jax.ShapeDtypeStruct((128, 512), f32),
            jax.ShapeDtypeStruct((2048, LANES), f32),
        ),
        in_specs=[vmem(), vmem(), hbm(), hbm(), hbm()],
        out_specs=(hbm(), vmem()),
        scratch_shapes=[
            pltpu.VMEM((512, 4096), jnp.bfloat16),
            pltpu.VMEM((4096, 256), jnp.bfloat16),
            pltpu.VMEM((128, 512), f32),
            pltpu.VMEM((128, 512), f32),
            pltpu.VMEM((128, 256), jnp.bfloat16),
            pltpu.VMEM((128, 512), f32),
            pltpu.SemaphoreType.DMA((3,)),
            pltpu.SemaphoreType.DMA(()),
        ],
        compiler_params=params(20),
        name="plates",
    )(arrived, cell, far(plate_temp), far(conductivity), far(jnp.asarray(plate_op)))


def finish(returned, position, wall_film, wall, t_new):
    f32 = jnp.float32
    count = wall.shape[1]
    return pl.pallas_call(
        finish_kernel,
        out_shape=(
            jax.ShapeDtypeStruct((8, 8, 8, count), f32),
            jax.ShapeDtypeStruct((128, count), f32),
        ),
        in_specs=[vmem(), vmem(), hbm(), hbm(), hbm()],
        out_specs=(hbm(), hbm()),
        scratch_shapes=[
            pltpu.SMEM((16, 128), jnp.int32),
            pltpu.VMEM((128, count), f32),
            pltpu.VMEM((128, count), f32),
            pltpu.VMEM((4096, LANES), f32),
            pltpu.VMEM((LANES, LANES), f32),
            pltpu.VMEM((128, count), f32),
            pltpu.VMEM((2, 8, 8, count), f32),
            pltpu.SemaphoreType.DMA((3,)),
            pltpu.SemaphoreType.DMA((8, 3)),
        ],
        input_output_aliases={4: 0},
        compiler_params=params(12),
        name="finish",
    )(returned, near(position), far(wall_film), far(wall), t_new)


def shards(warmth, velocity, wall_film, face_owner, plate_temp, conductivity, plate_cell):
    count = warmth.shape[1]
    axes = ("flow", "grp")
    devices = lax.axis_size(axes)

    def exchange(rows):
        return lax.all_to_all(rows, axes, split_axis=0, concat_axis=0, tiled=True)

    to_first, to_second = edges(warmth, velocity)
    pairs = [[(i, i + 1) for i in range(start, devices - 1, 2)] for start in (0, 1)]
    swaps = [forth + [(j, i) for i, j in forth] for forth in pairs]
    from_first = lax.ppermute(to_first, axes, swaps[0])
    from_second = lax.ppermute(to_second, axes, swaps[1])
    t, v = (x.reshape(8, 8, 8, count) for x in (warmth, velocity))
    *started, position = begin(t, v, wall_film, face_owner.reshape(16, 128))
    t_new, wall, sending = sweeps(*started, from_first, from_second, position)
    cell = plate_cell.reshape(32, LANES)
    arrived = exchange(sending.reshape(128, 32, LANES))
    sheet, returning = plates(arrived, cell, plate_temp, conductivity)
    returned = exchange(returning.reshape(128, 16, LANES)).reshape(2048, LANES)
    coolant, boundary = finish(returned, position, wall_film, wall, t_new)
    return coolant.reshape(512, count), boundary, sheet


def solution(mesh):
    placed = (
        P(None, ("flow", "grp")),
        P(None, ("flow", "grp")),
        P(None, ("flow", "grp")),
        P(("flow", "grp"), None),
        P(None, ("flow", "grp")),
        P(None, ("flow", "grp")),
        P(("flow", "grp")),
    )
    return jax.shard_map(
        shards,
        mesh=mesh,
        in_specs=placed,
        out_specs=(P(None, ("flow", "grp")), P(None, ("flow", "grp")), P(None, ("flow", "grp"))),
        check_vma=False,
    )
```

```python
import functools

import jax
import jax.numpy as jnp
import ml_dtypes
import numpy as np
from jax import lax
from jax.experimental import pallas as pl
from jax.experimental.pallas import tpu as pltpu
from jax.sharding import PartitionSpec as P

SWEEPS = 2
LAMBDA_H = 4.0
DAMPING_RATIO = 0.5
CARRY_STEP_SIZE = 0.05
CONTACT = 0.1
DT_PLATE = 0.0008
COUPLE = 20.0
MIXING_WEIGHT = 0.5
GLL_POINTS = (
    -1.0,
    -0.8717401485096066,
    -0.5917001814331423,
    -0.2092992179024789,
    0.2092992179024789,
    0.5917001814331423,
    0.8717401485096066,
    1.0,
)
GLL_WEIGHTS = (
    0.03571428571428571,
    0.2107042271435061,
    0.3411226924835044,
    0.4124587946587038,
    0.4124587946587038,
    0.3411226924835044,
    0.2107042271435061,
    0.03571428571428571,
)
LANES = 128


def split_pair(table):
    high = np.asarray(table, np.float32).astype(ml_dtypes.bfloat16)
    low = (np.asarray(table, np.float64) - high.astype(np.float64)).astype(np.float32)
    return high, low.astype(ml_dtypes.bfloat16)


def gll_tables():
    points = np.array(GLL_POINTS)
    weights = np.array(GLL_WEIGHTS)
    identity = np.eye(8)
    spread = points[:, None] - points[None, :] + identity
    bary_weight = 1.0 / np.prod(spread, axis=1)
    gradient = bary_weight[None, :] / bary_weight[:, None] / spread
    gradient = gradient * (1.0 - identity)
    gradient = gradient - identity * gradient.sum(axis=1)[:, None]
    stiffness = gradient.T * weights[None, :] @ gradient
    strong = stiffness / weights[:, None]
    ratio = np.diag(strong)
    laplace = (
        np.kron(np.kron(strong, identity), identity)
        + np.kron(np.kron(identity, strong), identity)
        + np.kron(np.kron(identity, identity), strong)
    )
    diagonal = (
        LAMBDA_H + ratio[:, None, None] + ratio[None, :, None] + ratio[None, None, :]
    ).reshape(512)
    share = np.ones((8, 64))
    share[0] = 0.5
    share[7] = 0.5
    smooth = -DAMPING_RATIO * (share.reshape(512) / diagonal)[:, None] * laplace
    quad = smooth.reshape(8, 64, 8, 64)
    near = quad[:4, :, :4, :]
    far = quad[:4, :, 7:3:-1, :]
    even = (0.5 * (near + far)).reshape(256, 256)
    odd = (0.5 * (near - far)).reshape(256, 256)
    carry = -CARRY_STEP_SIZE * gradient
    from_even = 0.5 * (carry[:4, :4] + carry[:4, 7:3:-1])
    from_odd = 0.5 * (carry[:4, :4] - carry[:4, 7:3:-1])
    weight_matrix = np.diag(weights)
    in_plane = (np.kron(stiffness, weight_matrix) + np.kron(weight_matrix, stiffness)) / np.kron(
        weights, weights
    )[:, None]
    through = np.array([[-1.0, 1.0], [1.0, -1.0]])
    plate_op = -np.kron(np.eye(2), in_plane) + COUPLE * np.kron(through, np.eye(64))
    even_parts = split_pair(even)
    odd_parts = split_pair(odd)
    smoothing = np.stack(
        [np.concatenate(even_parts, 1), np.concatenate(odd_parts, 1)]
    )
    plate_parts = np.concatenate(split_pair(plate_op), 1)
    return from_even, from_odd, smoothing, plate_parts


def halves(value):
    high = value.astype(jnp.bfloat16)
    low = (value - high.astype(jnp.float32)).astype(jnp.bfloat16)
    return high, low


def dot32(a, b):
    return jnp.dot(a, b, preferred_element_type=jnp.float32)


def edge_kernel(t_in, v_in, to_first, to_second, held, sems):
    count = t_in.shape[1]
    copies = []
    for i, array in enumerate((t_in, v_in)):
        for j, start in enumerate((0, count - LANES)):
            copy = pltpu.make_async_copy(
                array.at[:, pl.ds(start, LANES)], held.at[i, j], sems.at[i, j]
            )
            copy.start()
            copies.append(copy)
    for copy in copies:
        copy.wait()
    odd = lax.axis_index("grp") % 2 == 1
    for i in range(2):
        rows = pl.ds(2 * i, 2)
        bottom = held[i, 0].T[0:2, :]
        top = held[i, 1].T[126:128, :]
        to_first[rows, :] = jnp.where(odd, bottom, top)
        to_second[rows, :] = jnp.where(odd, top, bottom)
    to_first[4:8, :] = jnp.ones((4, 512), jnp.float32)
    to_second[4:8, :] = jnp.ones((4, 512), jnp.float32)


def fill_positions(owner, position):
    wide = 256
    row = lax.broadcasted_iota(jnp.int32, (wide, wide), 0)
    col = lax.broadcasted_iota(jnp.int32, (wide, wide), 1)
    upto = (row <= col).astype(jnp.float32).astype(jnp.bfloat16)
    name = lax.broadcasted_iota(jnp.int32, (128, LANES), 0)
    before = jnp.zeros((128, 1), jnp.float32)
    for step in range(8):
        pair = [
            (name == owner[2 * step + i : 2 * step + i + 1, :]).astype(jnp.float32)
            for i in range(2)
        ]
        hot = jnp.concatenate(pair, axis=1)
        seen = dot32(hot.astype(jnp.bfloat16), upto)
        rank = jnp.sum(hot * (seen + before), axis=0, keepdims=True) - 1.0
        before = before + seen[:, wide - 1 : wide]
        for i in range(2):
            at = slice(2 * step + i, 2 * step + i + 1)
            position[at, :] = owner[at, :] * 32 + rank[:, i * LANES : (i + 1) * LANES].astype(
                jnp.int32
            )


def carry(from_even, from_odd, start, v, adv, high, low, pair, block):
    lanes = pl.ds(block * LANES, LANES)
    parts = []
    for b in (2 * pair, 2 * pair + 1):
        t = start(b)
        e = [t[k] + t[7 - k] for k in range(4)]
        o = [t[k] - t[7 - k] for k in range(4)]
        kept = []
        for i in range(4):
            p = float(from_even[i, 0]) * e[0]
            q = float(from_odd[i, 0]) * o[0]
            for j in range(1, 4):
                p = p + float(from_even[i, j]) * e[j]
                q = q + float(from_odd[i, j]) * o[j]
            near = t[i] + v[i, b, :, lanes] * (q + p)
            far = t[7 - i] + v[7 - i, b, :, lanes] * (q - p)
            adv[i, b, :, lanes] = near
            adv[7 - i, b, :, lanes] = far
            kept.append((near + far, near - far))
        parts.append(kept)
    for i in range(4):
        for number in range(2):
            first, second = halves(
                jnp.concatenate([parts[0][i][number], parts[1][i][number]], axis=0)
            )
            rows = pl.ds(256 * number + 64 * i + 16 * pair, 16)
            high[rows, lanes] = first
            low[rows, lanes] = second


def smooth(smoothing, high, low, even, odd, group):
    lanes = pl.ds(group[0] * LANES, len(group) * LANES)
    for number, target in enumerate((even, odd)):
        rows = pl.ds(256 * number, 256)
        first = smoothing[number, :, pl.ds(0, 256)]
        second = smoothing[number, :, pl.ds(256, 256)]
        target[:, lanes] = (
            dot32(first, high[rows, lanes])
            + dot32(second, high[rows, lanes])
            + dot32(first, low[rows, lanes])
        )


def begin_kernel(
    from_even,
    from_odd,
    t,
    v_in,
    film_in,
    smoothing_in,
    owner,
    v,
    adv,
    even,
    odd,
    film,
    smoothing,
    position,
    cleared,
    high,
    low,
    sems,
):
    count = t.shape[-1]
    groups = [[2 * i, 2 * i + 1] for i in range(count // LANES // 2)]
    smoothing_copy = pltpu.make_async_copy(smoothing_in, smoothing, sems.at[0])
    film_copy = pltpu.make_async_copy(film_in, film, sems.at[1])
    v_copies = []
    for number, group in enumerate(groups):
        lanes = pl.ds(group[0] * LANES, 2 * LANES)
        v_copies.append(
            pltpu.make_async_copy(
                v_in.at[:, :, :, lanes], v.at[:, :, :, lanes], sems.at[2 + number]
            )
        )
    for copy in [v_copies[0], smoothing_copy] + v_copies[1:] + [film_copy]:
        copy.start()
    cleared[...] = jnp.zeros_like(cleared)
    fill_positions(owner, position)

    def advect(group):
        for pair in range(4):
            for block in group:
                lanes = pl.ds(block * LANES, LANES)
                carry(
                    from_even,
                    from_odd,
                    lambda b: [t[a, b, :, lanes] for a in range(8)],
                    v,
                    adv,
                    high,
                    low,
                    pair,
                    block,
                )

    v_copies[0].wait()
    advect(groups[0])
    smoothing_copy.wait()
    for copy in v_copies[1:]:
        copy.wait()
    for number in range(1, len(groups)):
        advect(groups[number])
        smooth(smoothing, high, low, even, odd, groups[number - 1])
    smooth(smoothing, high, low, even, odd, groups[-1])
    film_copy.wait()


def sweep_kernel(
    from_even,
    from_odd,
    v,
    adv,
    even_first,
    odd_first,
    film,
    smoothing,
    from_first,
    from_second,
    position_in,
    cleared,
    t_out,
    wall_out,
    sending,
    position,
    wall,
    t_edge,
    v_edge,
    adv_edge,
    high_edge,
    low_edge,
    even_edge,
    odd_edge,
    t_new,
    adv_second,
    high,
    low,
    even_second,
    odd_second,
    edge,
    faces,
    in_sem,
    out_sems,
):
    del cleared
    position_copy = pltpu.make_async_copy(position_in, position, in_sem)
    position_copy.start()
    count = v.shape[-1]
    inner = count // LANES
    blocks = inner + 1
    groups = [[2 * i, 2 * i + 1] for i in range(inner // 2)]
    odd = lax.axis_index("grp") % 2 == 1
    from_prev = jnp.where(odd, from_first[...], from_second[...])
    from_next = jnp.where(odd, from_second[...], from_first[...])
    edge[...] = jnp.zeros_like(edge)
    for i, array in enumerate((t_edge, v_edge)):
        edge[0:2, :] = from_next[2 * i : 2 * i + 2, :]
        edge[126:128, :] = from_prev[2 * i : 2 * i + 2, :]
        array[...] = edge[...].T.reshape(8, 8, 8, LANES)
    lane = lax.broadcasted_iota(jnp.int32, (8, LANES), 1)
    is_first = (lane == 0) & (from_prev[4:5, 0:LANES] == 0.0)
    is_last = (lane == LANES - 1) & (from_next[4:5, 0:LANES] == 0.0)

    changes = ((even_first, odd_first), (even_second, odd_second))

    def part(sweep, k, b, block):
        rows = pl.ds(64 * k + 8 * b, 8)
        if block == inner:
            return even_edge[sweep, rows, :], odd_edge[sweep, rows, :]
        even, odd = changes[sweep]
        lanes = pl.ds(block * LANES, LANES)
        return even[rows, lanes], odd[rows, lanes]

    def combine(sweep, start, b, block):
        e, o = part(sweep, 0, b, block)
        bottom, top = e + o, e - o
        e, o = part(sweep, 0, b, (block - 1) % blocks)
        before = pltpu.roll(jnp.where(lane == LANES - 1, e - o, top), 1, 1)
        e, o = part(sweep, 0, b, (block + 1) % blocks)
        after = pltpu.roll(jnp.where(lane == 0, e + o, bottom), LANES - 1, 1)
        if block == 0:
            before = jnp.where(is_first, bottom, before)
        if block == inner - 1:
            after = jnp.where(is_last, top, after)
        lanes = pl.ds((block % inner) * LANES, LANES)
        t = [None] * 8
        t[0] = start[0, b, :, lanes] + (bottom + before)
        t[7] = start[7, b, :, lanes] + (top + after)
        for k in range(1, 4):
            e, o = part(sweep, k, b, block)
            t[k] = start[k, b, :, lanes] + (e + o)
            t[7 - k] = start[7 - k, b, :, lanes] + (e - o)
        return t

    def carry_edge(sweep, start):
        into = adv_edge.at[sweep]
        for pair in range(4):
            carry(from_even, from_odd, start, v_edge, into, high_edge, low_edge, pair, 0)
        smooth(
            smoothing, high_edge, low_edge, even_edge.at[sweep], odd_edge.at[sweep], [0]
        )

    def carry_inner(group):
        for pair in range(4):
            for block in group:
                carry(
                    from_even,
                    from_odd,
                    functools.partial(combine, 0, adv, block=block),
                    v,
                    adv_second,
                    high,
                    low,
                    pair,
                    block,
                )

    stores = []

    def complete(number):
        group = groups[number]
        for block in group:
            lanes = pl.ds(block * LANES, LANES)
            for b in range(8):
                t = combine(1, adv_second, b, block)
                for a in range(8):
                    t_new[a, b, :, lanes] = t[a]
            for side in range(2):
                own = t_new[:, 7 * side, :, lanes].reshape(64, LANES)
                wall[pl.ds(64 * side, 64), lanes] = own
                layer = film[pl.ds(64 * side, 64), lanes]
                faces[side, lanes, :] = jnp.concatenate([layer, layer * own], axis=0).T
            for j in range(2 * LANES):
                spot = position[2 * block + j // LANES, j % LANES]
                sending[pl.ds(spot, 1), :] = faces[j % 2, pl.ds(block * LANES + j // 2, 1), :]
        lanes = pl.ds(group[0] * LANES, 2 * LANES)
        copy = pltpu.make_async_copy(
            t_new.at[:, :, :, lanes], t_out.at[:, :, :, lanes], out_sems.at[number]
        )
        copy.start()
        stores.append(copy)

    carry_edge(0, lambda b: [t_edge[a, b, :, :] for a in range(8)])
    carry_inner(groups[0])
    carry_edge(1, functools.partial(combine, 0, adv_edge.at[0], block=inner))
    position_copy.wait()
    smooth(smoothing, high, low, even_second, odd_second, groups[0])
    for number in range(1, len(groups)):
        carry_inner(groups[number])
        smooth(smoothing, high, low, even_second, odd_second, groups[number])
        if number > 1:
            complete(number - 2)
    complete(len(groups) - 2)
    complete(len(groups) - 1)
    copy = pltpu.make_async_copy(wall, wall_out, out_sems.at[4])
    copy.start()
    stores.append(copy)
    for copy in stores:
        copy.wait()


def owner_kernel(
    arrived,
    cell,
    plate_in,
    conductivity_in,
    plate_op_in,
    sheet_out,
    returning,
    hot,
    parts,
    plate,
    conductivity,
    plate_op,
    sheet,
    in_sems,
    out_sem,
):
    loads = [
        pltpu.make_async_copy(plate_in, plate, in_sems.at[0]),
        pltpu.make_async_copy(conductivity_in, conductivity, in_sems.at[1]),
        pltpu.make_async_copy(plate_op_in, plate_op, in_sems.at[2]),
    ]
    for copy in loads:
        copy.start()
    lane = lax.broadcasted_iota(jnp.int32, (16, LANES), 1)
    cells = []
    for half in range(2):
        ordered = jnp.zeros((16, LANES), jnp.int32)
        for i in range(8):
            own = cell[pl.ds(i // 4, 16, stride=2), :]
            shift = (16 * i - 32 * (i % 4) - 16 * half) % LANES
            moved = pltpu.roll(own, shift, 1) if shift else own
            ordered = jnp.where(lane // 16 == i, moved, ordered)
        cells.append(ordered.astype(jnp.int16))
    name = lax.broadcasted_iota(jnp.int32, (512, LANES), 0).astype(jnp.int16)
    one, zero = jnp.bfloat16(1), jnp.bfloat16(0)
    both = [None, None]
    for chunk in range(4):
        for i in range(8):
            place = 8 * chunk + i
            block = arrived[
                pl.ds(8 * (place % 16), 8), pl.ds(16 * (place // 16), 16), :
            ].reshape(128, LANES)
            first, second = halves(block)
            rows = pl.ds(place * 128, 128)
            parts[rows, pl.ds(0, LANES)] = first
            parts[rows, pl.ds(LANES, LANES)] = second
            hot[:, rows] = jnp.where(
                name == cells[place // 16][place % 16 : place % 16 + 1, :], one, zero
            )
        slots = pl.ds(1024 * chunk, 1024)
        for i in range(2):
            share = dot32(hot[pl.ds(256 * i, 256), slots], parts[slots, :])
            both[i] = share if chunk == 0 else both[i] + share
    both = jnp.concatenate(both, axis=0)
    total = (both[:, :LANES] + both[:, LANES:]).T
    film_sum = total[:64]
    heat_sum = total[64:]
    for copy in loads:
        copy.wait()
    contact = (plate[0:64, :] + CONTACT * heat_sum) / (1.0 + CONTACT * film_sum)
    relaxed = jnp.concatenate([contact, plate[64:128, :]], axis=0)
    first, second = halves(relaxed)
    op_first = plate_op[:, pl.ds(0, 128)]
    op_second = plate_op[:, pl.ds(128, 128)]
    spread = dot32(op_first, first) + dot32(op_second, first) + dot32(op_first, second)
    conducted = relaxed + DT_PLATE * conductivity[...] * spread
    sheet[...] = conducted
    store = pltpu.make_async_copy(sheet, sheet_out, out_sem)
    store.start()
    first, second = halves(conducted[:64])
    mixed = jnp.concatenate([first, second], axis=0)
    for chunk in range(4):
        seen = []
        for half in range(2):
            both_parts = dot32(mixed, hot[:, pl.ds(2048 * half + 512 * chunk, 512)])
            seen.append(both_parts[:64] + both_parts[64:])
        for i in range(4):
            slots = slice(i * 128, (i + 1) * 128)
            block = jnp.concatenate([seen[0][:, slots], seen[1][:, slots]], axis=0)
            returning[pl.ds(512 * chunk + i * 128, 128), :] = block.T
    store.wait()


def finish_kernel(
    returned,
    position_in,
    film_in,
    wall_in,
    t_in,
    t_out,
    contact_out,
    position,
    film,
    wall,
    rows,
    gathered,
    contact,
    out,
    in_sems,
    out_sems,
):
    del t_in
    loads = [
        pltpu.make_async_copy(position_in, position, in_sems.at[0]),
        pltpu.make_async_copy(film_in, film, in_sems.at[1]),
        pltpu.make_async_copy(wall_in, wall, in_sems.at[2]),
    ]
    for copy in loads:
        copy.start()
    lane = lax.broadcasted_iota(jnp.int32, (16, LANES), 1)

    def expand(i, _):
        for k in range(32):
            block = returned[pl.ds(512 * i + 16 * k, 16), :]
            turned = pltpu.roll(block, 64, 1)
            at = 1024 * i + 32 * k
            rows[pl.ds(at, 16), :] = jnp.where(lane < 64, block, turned)
            rows[pl.ds(at + 16, 16), :] = jnp.where(lane < 64, turned, block)
        return 0

    lax.fori_loop(0, 4, expand, 0)
    loads[0].wait()
    one = lax.broadcasted_iota(jnp.int32, (1, LANES), 1)
    stores = []
    for block in range(8):
        for j in range(LANES):
            i, k = 2 * block + j // 64, 2 * (j % 64)
            low = rows[pl.ds(position[i, k], 1), :]
            high = rows[pl.ds(position[i, k + 1], 1), :]
            gathered[pl.ds(j, 1), :] = jnp.where(one < 64, low, high)
        if block == 0:
            loads[1].wait()
            loads[2].wait()
        lanes = pl.ds(block * LANES, LANES)
        seen = gathered[...].T
        contact[:, lanes] = seen
        own = wall[:, lanes]
        out[:, :, :, lanes] = (
            own + MIXING_WEIGHT * (film[:, lanes] * (seen - own))
        ).reshape(2, 8, 8, LANES)
        copies = [
            pltpu.make_async_copy(
                contact.at[:, lanes], contact_out.at[:, lanes], out_sems.at[block, 0]
            )
        ] + [
            pltpu.make_async_copy(
                out.at[side, :, :, lanes], t_out.at[:, 7 * side, :, lanes], out_sems.at[block, 1 + side]
            )
            for side in range(2)
        ]
        for copy in copies:
            copy.start()
        stores += copies
    for copy in stores:
        copy.wait()


def vmem():
    return pl.BlockSpec(memory_space=pltpu.VMEM)


def smem():
    return pl.BlockSpec(memory_space=pltpu.SMEM)


def hbm():
    return pl.BlockSpec(memory_space=pltpu.HBM)


def far(array):
    return pltpu.with_memory_space_constraint(array, pltpu.HBM)


def params(mebibytes):
    return pltpu.CompilerParams(vmem_limit_bytes=mebibytes * 1024 * 1024)


def edges(warmth, velocity):
    side = jax.ShapeDtypeStruct((8, 512), jnp.float32)
    return pl.pallas_call(
        edge_kernel,
        out_shape=(side, side),
        in_specs=[hbm(), hbm()],
        out_specs=(vmem(), vmem()),
        scratch_shapes=[
            pltpu.VMEM((2, 2, 512, LANES), jnp.float32),
            pltpu.SemaphoreType.DMA((2, 2)),
        ],
        compiler_params=params(4),
        name="edges",
    )(far(warmth), far(velocity))


def near(array):
    return pltpu.with_memory_space_constraint(array, pltpu.VMEM)


def begin(t, v, wall_film, owner):
    f32 = jnp.float32
    from_even, from_odd, smoothing, _ = gll_tables()
    count = t.shape[-1]
    return pl.pallas_call(
        functools.partial(begin_kernel, from_even, from_odd),
        out_shape=(
            pltpu.VMEM((8, 8, 8, count), f32),
            pltpu.VMEM((8, 8, 8, count), f32),
            pltpu.VMEM((256, count), f32),
            pltpu.VMEM((256, count), f32),
            pltpu.VMEM((128, count), f32),
            pltpu.VMEM((2, 256, 512), jnp.bfloat16),
            jax.ShapeDtypeStruct((16, 128), jnp.int32),
            pltpu.VMEM((4096, LANES), f32),
        ),
        in_specs=[vmem(), hbm(), hbm(), hbm(), vmem()],
        out_specs=(vmem(),) * 8,
        scratch_shapes=[
            pltpu.VMEM((512, count), jnp.bfloat16),
            pltpu.VMEM((512, count), jnp.bfloat16),
            pltpu.SemaphoreType.DMA((6,)),
        ],
        compiler_params=params(20),
        name="begin",
    )(near(t), far(v), far(wall_film), far(jnp.asarray(smoothing)), owner)


def sweeps(v, adv, even, odd, film, smoothing, from_first, from_second, position, cleared):
    f32 = jnp.float32
    bf16 = jnp.bfloat16
    from_even, from_odd, _, _ = gll_tables()
    count = v.shape[-1]
    held = [near(x) for x in (v, adv, even, odd, film, smoothing)]
    return pl.pallas_call(
        functools.partial(sweep_kernel, from_even, from_odd),
        out_shape=(
            jax.ShapeDtypeStruct((8, 8, 8, count), f32),
            pltpu.HBM((128, count), f32),
            pltpu.VMEM((4096, LANES), f32),
        ),
        in_specs=[vmem()] * 8 + [hbm(), vmem()],
        out_specs=(hbm(), hbm(), vmem()),
        scratch_shapes=[
            pltpu.SMEM((16, 128), jnp.int32),
            pltpu.VMEM((128, count), f32),
            pltpu.VMEM((8, 8, 8, LANES), f32),
            pltpu.VMEM((8, 8, 8, LANES), f32),
            pltpu.VMEM((2, 8, 8, 8, LANES), f32),
            pltpu.VMEM((512, LANES), bf16),
            pltpu.VMEM((512, LANES), bf16),
            pltpu.VMEM((2, 256, LANES), f32),
            pltpu.VMEM((2, 256, LANES), f32),
            pltpu.VMEM((8, 8, 8, count), f32),
            pltpu.VMEM((8, 8, 8, count), f32),
            pltpu.VMEM((512, count), bf16),
            pltpu.VMEM((512, count), bf16),
            pltpu.VMEM((256, count), f32),
            pltpu.VMEM((256, count), f32),
            pltpu.VMEM((128, 512), f32),
            pltpu.VMEM((2, count, LANES), f32),
            pltpu.SemaphoreType.DMA(()),
            pltpu.SemaphoreType.DMA((5,)),
        ],
        input_output_aliases={9: 2},
        compiler_params=params(28),
        name="sweeps",
    )(*held, from_first, from_second, position, near(cleared))


def plates(arrived, cell, plate_temp, conductivity):
    f32 = jnp.float32
    plate_op = gll_tables()[3]
    return pl.pallas_call(
        owner_kernel,
        out_shape=(
            jax.ShapeDtypeStruct((128, 512), f32),
            jax.ShapeDtypeStruct((2048, LANES), f32),
        ),
        in_specs=[vmem(), vmem(), hbm(), hbm(), hbm()],
        out_specs=(hbm(), vmem()),
        scratch_shapes=[
            pltpu.VMEM((512, 4096), jnp.bfloat16),
            pltpu.VMEM((4096, 256), jnp.bfloat16),
            pltpu.VMEM((128, 512), f32),
            pltpu.VMEM((128, 512), f32),
            pltpu.VMEM((128, 256), jnp.bfloat16),
            pltpu.VMEM((128, 512), f32),
            pltpu.SemaphoreType.DMA((3,)),
            pltpu.SemaphoreType.DMA(()),
        ],
        compiler_params=params(20),
        name="plates",
    )(arrived, cell, far(plate_temp), far(conductivity), far(jnp.asarray(plate_op)))


def finish(returned, position, wall_film, wall, t_new):
    f32 = jnp.float32
    count = wall.shape[1]
    return pl.pallas_call(
        finish_kernel,
        out_shape=(
            jax.ShapeDtypeStruct((8, 8, 8, count), f32),
            jax.ShapeDtypeStruct((128, count), f32),
        ),
        in_specs=[vmem(), vmem(), hbm(), hbm(), hbm()],
        out_specs=(hbm(), hbm()),
        scratch_shapes=[
            pltpu.SMEM((16, 128), jnp.int32),
            pltpu.VMEM((128, count), f32),
            pltpu.VMEM((128, count), f32),
            pltpu.VMEM((4096, LANES), f32),
            pltpu.VMEM((LANES, LANES), f32),
            pltpu.VMEM((128, count), f32),
            pltpu.VMEM((2, 8, 8, count), f32),
            pltpu.SemaphoreType.DMA((3,)),
            pltpu.SemaphoreType.DMA((8, 3)),
        ],
        input_output_aliases={4: 0},
        compiler_params=params(12),
        name="finish",
    )(returned, near(position), far(wall_film), far(wall), t_new)


def shards(warmth, velocity, wall_film, face_owner, plate_temp, conductivity, plate_cell):
    count = warmth.shape[1]
    axes = ("flow", "grp")
    devices = lax.axis_size(axes)

    def exchange(rows):
        return lax.all_to_all(rows, axes, split_axis=0, concat_axis=0, tiled=True)

    to_first, to_second = edges(warmth, velocity)
    pairs = [[(i, i + 1) for i in range(start, devices - 1, 2)] for start in (0, 1)]
    swaps = [forth + [(j, i) for i, j in forth] for forth in pairs]
    from_first = lax.ppermute(to_first, axes, swaps[0])
    from_second = lax.ppermute(to_second, axes, swaps[1])
    t, v = (x.reshape(8, 8, 8, count) for x in (warmth, velocity))
    *started, position, cleared = begin(t, v, wall_film, face_owner.reshape(16, 128))
    t_new, wall, sending = sweeps(*started, from_first, from_second, position, cleared)
    cell = plate_cell.reshape(32, LANES)
    arrived = exchange(sending.reshape(128, 32, LANES))
    sheet, returning = plates(arrived, cell, plate_temp, conductivity)
    returned = exchange(returning.reshape(128, 16, LANES)).reshape(2048, LANES)
    coolant, boundary = finish(returned, position, wall_film, wall, t_new)
    return coolant.reshape(512, count), boundary, sheet


def solution(mesh):
    placed = (
        P(None, ("flow", "grp")),
        P(None, ("flow", "grp")),
        P(None, ("flow", "grp")),
        P(("flow", "grp"), None),
        P(None, ("flow", "grp")),
        P(None, ("flow", "grp")),
        P(("flow", "grp")),
    )
    return jax.shard_map(
        shards,
        mesh=mesh,
        in_specs=placed,
        out_specs=(P(None, ("flow", "grp")), P(None, ("flow", "grp")), P(None, ("flow", "grp"))),
        check_vma=False,
    )
```

```python
import functools

import jax
import jax.numpy as jnp
import ml_dtypes
import numpy as np
from jax import lax
from jax.experimental import pallas as pl
from jax.experimental.pallas import tpu as pltpu
from jax.sharding import PartitionSpec as P

SWEEPS = 2
LAMBDA_H = 4.0
DAMPING_RATIO = 0.5
CARRY_STEP_SIZE = 0.05
CONTACT = 0.1
DT_PLATE = 0.0008
COUPLE = 20.0
MIXING_WEIGHT = 0.5
GLL_POINTS = (
    -1.0,
    -0.8717401485096066,
    -0.5917001814331423,
    -0.2092992179024789,
    0.2092992179024789,
    0.5917001814331423,
    0.8717401485096066,
    1.0,
)
GLL_WEIGHTS = (
    0.03571428571428571,
    0.2107042271435061,
    0.3411226924835044,
    0.4124587946587038,
    0.4124587946587038,
    0.3411226924835044,
    0.2107042271435061,
    0.03571428571428571,
)
LANES = 128


def split_pair(table):
    high = np.asarray(table, np.float32).astype(ml_dtypes.bfloat16)
    low = (np.asarray(table, np.float64) - high.astype(np.float64)).astype(np.float32)
    return high, low.astype(ml_dtypes.bfloat16)


def gll_tables():
    points = np.array(GLL_POINTS)
    weights = np.array(GLL_WEIGHTS)
    identity = np.eye(8)
    spread = points[:, None] - points[None, :] + identity
    bary_weight = 1.0 / np.prod(spread, axis=1)
    gradient = bary_weight[None, :] / bary_weight[:, None] / spread
    gradient = gradient * (1.0 - identity)
    gradient = gradient - identity * gradient.sum(axis=1)[:, None]
    stiffness = gradient.T * weights[None, :] @ gradient
    strong = stiffness / weights[:, None]
    ratio = np.diag(strong)
    laplace = (
        np.kron(np.kron(strong, identity), identity)
        + np.kron(np.kron(identity, strong), identity)
        + np.kron(np.kron(identity, identity), strong)
    )
    diagonal = (
        LAMBDA_H + ratio[:, None, None] + ratio[None, :, None] + ratio[None, None, :]
    ).reshape(512)
    share = np.ones((8, 64))
    share[0] = 0.5
    share[7] = 0.5
    smooth = -DAMPING_RATIO * (share.reshape(512) / diagonal)[:, None] * laplace
    quad = smooth.reshape(8, 64, 8, 64)
    near = quad[:4, :, :4, :]
    far = quad[:4, :, 7:3:-1, :]
    even = (0.5 * (near + far)).reshape(256, 256)
    odd = (0.5 * (near - far)).reshape(256, 256)
    carry = -CARRY_STEP_SIZE * gradient
    from_even = 0.5 * (carry[:4, :4] + carry[:4, 7:3:-1])
    from_odd = 0.5 * (carry[:4, :4] - carry[:4, 7:3:-1])
    weight_matrix = np.diag(weights)
    in_plane = (np.kron(stiffness, weight_matrix) + np.kron(weight_matrix, stiffness)) / np.kron(
        weights, weights
    )[:, None]
    through = np.array([[-1.0, 1.0], [1.0, -1.0]])
    plate_op = -np.kron(np.eye(2), in_plane) + COUPLE * np.kron(through, np.eye(64))
    even_parts = split_pair(even)
    odd_parts = split_pair(odd)
    smoothing = np.stack(
        [np.concatenate(even_parts, 1), np.concatenate(odd_parts, 1)]
    )
    plate_parts = np.concatenate(split_pair(plate_op), 1)
    return from_even, from_odd, smoothing, plate_parts


def halves(value):
    high = value.astype(jnp.bfloat16)
    low = (value - high.astype(jnp.float32)).astype(jnp.bfloat16)
    return high, low


def dot32(a, b):
    return jnp.dot(a, b, preferred_element_type=jnp.float32)


def edge_kernel(t_in, v_in, to_first, to_second, held, sems):
    count = t_in.shape[1]
    copies = []
    for i, array in enumerate((t_in, v_in)):
        for j, start in enumerate((0, count - LANES)):
            copy = pltpu.make_async_copy(
                array.at[:, pl.ds(start, LANES)], held.at[i, j], sems.at[i, j]
            )
            copy.start()
            copies.append(copy)
    for copy in copies:
        copy.wait()
    odd = lax.axis_index("grp") % 2 == 1
    for i in range(2):
        rows = pl.ds(2 * i, 2)
        bottom = held[i, 0].T[0:2, :]
        top = held[i, 1].T[126:128, :]
        to_first[rows, :] = jnp.where(odd, bottom, top)
        to_second[rows, :] = jnp.where(odd, top, bottom)
    to_first[4:8, :] = jnp.ones((4, 512), jnp.float32)
    to_second[4:8, :] = jnp.ones((4, 512), jnp.float32)


def fill_positions(owner, position):
    wide = 256
    row = lax.broadcasted_iota(jnp.int32, (wide, wide), 0)
    col = lax.broadcasted_iota(jnp.int32, (wide, wide), 1)
    upto = (row <= col).astype(jnp.float32).astype(jnp.bfloat16)
    name = lax.broadcasted_iota(jnp.int32, (128, LANES), 0)
    before = jnp.zeros((128, 1), jnp.float32)
    for step in range(8):
        pair = [
            (name == owner[2 * step + i : 2 * step + i + 1, :]).astype(jnp.float32)
            for i in range(2)
        ]
        hot = jnp.concatenate(pair, axis=1)
        seen = dot32(hot.astype(jnp.bfloat16), upto)
        rank = jnp.sum(hot * (seen + before), axis=0, keepdims=True) - 1.0
        before = before + seen[:, wide - 1 : wide]
        for i in range(2):
            at = slice(2 * step + i, 2 * step + i + 1)
            position[at, :] = owner[at, :] * 32 + rank[:, i * LANES : (i + 1) * LANES].astype(
                jnp.int32
            )


def carry(from_even, from_odd, start, v, adv, high, low, pair, block):
    lanes = pl.ds(block * LANES, LANES)
    parts = []
    for b in (2 * pair, 2 * pair + 1):
        t = start(b)
        e = [t[k] + t[7 - k] for k in range(4)]
        o = [t[k] - t[7 - k] for k in range(4)]
        kept = []
        for i in range(4):
            p = float(from_even[i, 0]) * e[0]
            q = float(from_odd[i, 0]) * o[0]
            for j in range(1, 4):
                p = p + float(from_even[i, j]) * e[j]
                q = q + float(from_odd[i, j]) * o[j]
            near = t[i] + v[i, b, :, lanes] * (q + p)
            far = t[7 - i] + v[7 - i, b, :, lanes] * (q - p)
            adv[i, b, :, lanes] = near
            adv[7 - i, b, :, lanes] = far
            kept.append((near + far, near - far))
        parts.append(kept)
    for i in range(4):
        for number in range(2):
            first, second = halves(
                jnp.concatenate([parts[0][i][number], parts[1][i][number]], axis=0)
            )
            rows = pl.ds(256 * number + 64 * i + 16 * pair, 16)
            high[rows, lanes] = first
            low[rows, lanes] = second


def smooth(smoothing, high, low, even, odd, group):
    lanes = pl.ds(group[0] * LANES, len(group) * LANES)
    for number, target in enumerate((even, odd)):
        rows = pl.ds(256 * number, 256)
        first = smoothing[number, :, pl.ds(0, 256)]
        second = smoothing[number, :, pl.ds(256, 256)]
        target[:, lanes] = (
            dot32(first, high[rows, lanes])
            + dot32(second, high[rows, lanes])
            + dot32(first, low[rows, lanes])
        )


def begin_kernel(
    from_even,
    from_odd,
    t,
    v_in,
    smoothing_in,
    owner,
    v,
    adv,
    even,
    odd,
    smoothing,
    position,
    cleared,
    high,
    low,
    sems,
):
    count = t.shape[-1]
    groups = [[2 * i, 2 * i + 1] for i in range(count // LANES // 2)]
    smoothing_copy = pltpu.make_async_copy(smoothing_in, smoothing, sems.at[0])
    v_copies = []
    for number, group in enumerate(groups):
        lanes = pl.ds(group[0] * LANES, 2 * LANES)
        v_copies.append(
            pltpu.make_async_copy(
                v_in.at[:, :, :, lanes], v.at[:, :, :, lanes], sems.at[2 + number]
            )
        )
    for copy in [v_copies[0], smoothing_copy] + v_copies[1:]:
        copy.start()
    cleared[...] = jnp.zeros_like(cleared)
    fill_positions(owner, position)

    def advect(group):
        for pair in range(4):
            for block in group:
                lanes = pl.ds(block * LANES, LANES)
                carry(
                    from_even,
                    from_odd,
                    lambda b: [t[a, b, :, lanes] for a in range(8)],
                    v,
                    adv,
                    high,
                    low,
                    pair,
                    block,
                )

    v_copies[0].wait()
    advect(groups[0])
    smoothing_copy.wait()
    for copy in v_copies[1:]:
        copy.wait()
    for number in range(1, len(groups)):
        advect(groups[number])
        smooth(smoothing, high, low, even, odd, groups[number - 1])
    smooth(smoothing, high, low, even, odd, groups[-1])


def sweep_kernel(
    from_even,
    from_odd,
    v,
    adv,
    even_first,
    odd_first,
    film_in,
    smoothing,
    from_first,
    from_second,
    position_in,
    cleared,
    t_out,
    wall_out,
    sending,
    position,
    film,
    wall,
    t_edge,
    v_edge,
    adv_edge,
    high_edge,
    low_edge,
    even_edge,
    odd_edge,
    t_new,
    adv_second,
    high,
    low,
    even_second,
    odd_second,
    edge,
    faces,
    in_sem,
    out_sems,
):
    del cleared
    position_copy = pltpu.make_async_copy(position_in, position, in_sem)
    position_copy.start()
    film_copy = pltpu.make_async_copy(film_in, film, out_sems.at[5])
    film_copy.start()
    count = v.shape[-1]
    inner = count // LANES
    blocks = inner + 1
    groups = [[2 * i, 2 * i + 1] for i in range(inner // 2)]
    odd = lax.axis_index("grp") % 2 == 1
    from_prev = jnp.where(odd, from_first[...], from_second[...])
    from_next = jnp.where(odd, from_second[...], from_first[...])
    edge[...] = jnp.zeros_like(edge)
    for i, array in enumerate((t_edge, v_edge)):
        edge[0:2, :] = from_next[2 * i : 2 * i + 2, :]
        edge[126:128, :] = from_prev[2 * i : 2 * i + 2, :]
        array[...] = edge[...].T.reshape(8, 8, 8, LANES)
    lane = lax.broadcasted_iota(jnp.int32, (8, LANES), 1)
    is_first = (lane == 0) & (from_prev[4:5, 0:LANES] == 0.0)
    is_last = (lane == LANES - 1) & (from_next[4:5, 0:LANES] == 0.0)

    changes = ((even_first, odd_first), (even_second, odd_second))

    def part(sweep, k, b, block):
        rows = pl.ds(64 * k + 8 * b, 8)
        if block == inner:
            return even_edge[sweep, rows, :], odd_edge[sweep, rows, :]
        even, odd = changes[sweep]
        lanes = pl.ds(block * LANES, LANES)
        return even[rows, lanes], odd[rows, lanes]

    def combine(sweep, start, b, block):
        e, o = part(sweep, 0, b, block)
        bottom, top = e + o, e - o
        e, o = part(sweep, 0, b, (block - 1) % blocks)
        before = pltpu.roll(jnp.where(lane == LANES - 1, e - o, top), 1, 1)
        e, o = part(sweep, 0, b, (block + 1) % blocks)
        after = pltpu.roll(jnp.where(lane == 0, e + o, bottom), LANES - 1, 1)
        if block == 0:
            before = jnp.where(is_first, bottom, before)
        if block == inner - 1:
            after = jnp.where(is_last, top, after)
        lanes = pl.ds((block % inner) * LANES, LANES)
        t = [None] * 8
        t[0] = start[0, b, :, lanes] + (bottom + before)
        t[7] = start[7, b, :, lanes] + (top + after)
        for k in range(1, 4):
            e, o = part(sweep, k, b, block)
            t[k] = start[k, b, :, lanes] + (e + o)
            t[7 - k] = start[7 - k, b, :, lanes] + (e - o)
        return t

    def carry_edge(sweep, start):
        into = adv_edge.at[sweep]
        for pair in range(4):
            carry(from_even, from_odd, start, v_edge, into, high_edge, low_edge, pair, 0)
        smooth(
            smoothing, high_edge, low_edge, even_edge.at[sweep], odd_edge.at[sweep], [0]
        )

    def carry_inner(group):
        for pair in range(4):
            for block in group:
                carry(
                    from_even,
                    from_odd,
                    functools.partial(combine, 0, adv, block=block),
                    v,
                    adv_second,
                    high,
                    low,
                    pair,
                    block,
                )

    stores = []

    def complete(number):
        group = groups[number]
        for block in group:
            lanes = pl.ds(block * LANES, LANES)
            for b in range(8):
                t = combine(1, adv_second, b, block)
                for a in range(8):
                    t_new[a, b, :, lanes] = t[a]
            for side in range(2):
                own = t_new[:, 7 * side, :, lanes].reshape(64, LANES)
                wall[pl.ds(64 * side, 64), lanes] = own
                layer = film[pl.ds(64 * side, 64), lanes]
                faces[side, lanes, :] = jnp.concatenate([layer, layer * own], axis=0).T
            for j in range(2 * LANES):
                spot = position[2 * block + j // LANES, j % LANES]
                sending[pl.ds(spot, 1), :] = faces[j % 2, pl.ds(block * LANES + j // 2, 1), :]
        lanes = pl.ds(group[0] * LANES, 2 * LANES)
        copy = pltpu.make_async_copy(
            t_new.at[:, :, :, lanes], t_out.at[:, :, :, lanes], out_sems.at[number]
        )
        copy.start()
        stores.append(copy)

    carry_edge(0, lambda b: [t_edge[a, b, :, :] for a in range(8)])
    carry_inner(groups[0])
    carry_edge(1, functools.partial(combine, 0, adv_edge.at[0], block=inner))
    position_copy.wait()
    film_copy.wait()
    smooth(smoothing, high, low, even_second, odd_second, groups[0])
    for number in range(1, len(groups)):
        carry_inner(groups[number])
        smooth(smoothing, high, low, even_second, odd_second, groups[number])
        if number > 1:
            complete(number - 2)
    complete(len(groups) - 2)
    complete(len(groups) - 1)
    copy = pltpu.make_async_copy(wall, wall_out, out_sems.at[4])
    copy.start()
    stores.append(copy)
    for copy in stores:
        copy.wait()


def owner_kernel(
    arrived,
    cell,
    plate_in,
    conductivity_in,
    plate_op_in,
    sheet_out,
    returning,
    hot,
    parts,
    plate,
    conductivity,
    plate_op,
    sheet,
    in_sems,
    out_sem,
):
    loads = [
        pltpu.make_async_copy(plate_in, plate, in_sems.at[0]),
        pltpu.make_async_copy(conductivity_in, conductivity, in_sems.at[1]),
        pltpu.make_async_copy(plate_op_in, plate_op, in_sems.at[2]),
    ]
    for copy in loads:
        copy.start()
    lane = lax.broadcasted_iota(jnp.int32, (16, LANES), 1)
    cells = []
    for half in range(2):
        ordered = jnp.zeros((16, LANES), jnp.int32)
        for i in range(8):
            own = cell[pl.ds(i // 4, 16, stride=2), :]
            shift = (16 * i - 32 * (i % 4) - 16 * half) % LANES
            moved = pltpu.roll(own, shift, 1) if shift else own
            ordered = jnp.where(lane // 16 == i, moved, ordered)
        cells.append(ordered.astype(jnp.int16))
    name = lax.broadcasted_iota(jnp.int32, (512, LANES), 0).astype(jnp.int16)
    one, zero = jnp.bfloat16(1), jnp.bfloat16(0)
    both = [None, None]
    for chunk in range(4):
        for i in range(8):
            place = 8 * chunk + i
            block = arrived[
                pl.ds(8 * (place % 16), 8), pl.ds(16 * (place // 16), 16), :
            ].reshape(128, LANES)
            first, second = halves(block)
            rows = pl.ds(place * 128, 128)
            parts[rows, pl.ds(0, LANES)] = first
            parts[rows, pl.ds(LANES, LANES)] = second
            hot[:, rows] = jnp.where(
                name == cells[place // 16][place % 16 : place % 16 + 1, :], one, zero
            )
        slots = pl.ds(1024 * chunk, 1024)
        for i in range(2):
            share = dot32(hot[pl.ds(256 * i, 256), slots], parts[slots, :])
            both[i] = share if chunk == 0 else both[i] + share
    both = jnp.concatenate(both, axis=0)
    total = (both[:, :LANES] + both[:, LANES:]).T
    film_sum = total[:64]
    heat_sum = total[64:]
    for copy in loads:
        copy.wait()
    contact = (plate[0:64, :] + CONTACT * heat_sum) / (1.0 + CONTACT * film_sum)
    relaxed = jnp.concatenate([contact, plate[64:128, :]], axis=0)
    first, second = halves(relaxed)
    op_first = plate_op[:, pl.ds(0, 128)]
    op_second = plate_op[:, pl.ds(128, 128)]
    spread = dot32(op_first, first) + dot32(op_second, first) + dot32(op_first, second)
    conducted = relaxed + DT_PLATE * conductivity[...] * spread
    sheet[...] = conducted
    store = pltpu.make_async_copy(sheet, sheet_out, out_sem)
    store.start()
    first, second = halves(conducted[:64])
    mixed = jnp.concatenate([first, second], axis=0)
    for chunk in range(4):
        seen = []
        for half in range(2):
            both_parts = dot32(mixed, hot[:, pl.ds(2048 * half + 512 * chunk, 512)])
            seen.append(both_parts[:64] + both_parts[64:])
        for i in range(4):
            slots = slice(i * 128, (i + 1) * 128)
            block = jnp.concatenate([seen[0][:, slots], seen[1][:, slots]], axis=0)
            returning[pl.ds(512 * chunk + i * 128, 128), :] = block.T
    store.wait()


def finish_kernel(
    returned,
    position_in,
    film_in,
    wall_in,
    t_in,
    t_out,
    contact_out,
    position,
    film,
    wall,
    rows,
    gathered,
    contact,
    out,
    in_sems,
    out_sems,
):
    del t_in
    loads = [
        pltpu.make_async_copy(position_in, position, in_sems.at[0]),
        pltpu.make_async_copy(film_in, film, in_sems.at[1]),
        pltpu.make_async_copy(wall_in, wall, in_sems.at[2]),
    ]
    for copy in loads:
        copy.start()
    lane = lax.broadcasted_iota(jnp.int32, (16, LANES), 1)

    def expand(i, _):
        for k in range(32):
            block = returned[pl.ds(512 * i + 16 * k, 16), :]
            turned = pltpu.roll(block, 64, 1)
            at = 1024 * i + 32 * k
            rows[pl.ds(at, 16), :] = jnp.where(lane < 64, block, turned)
            rows[pl.ds(at + 16, 16), :] = jnp.where(lane < 64, turned, block)
        return 0

    lax.fori_loop(0, 4, expand, 0)
    loads[0].wait()
    one = lax.broadcasted_iota(jnp.int32, (1, LANES), 1)
    stores = []
    for block in range(8):
        for j in range(LANES):
            i, k = 2 * block + j // 64, 2 * (j % 64)
            low = rows[pl.ds(position[i, k], 1), :]
            high = rows[pl.ds(position[i, k + 1], 1), :]
            gathered[pl.ds(j, 1), :] = jnp.where(one < 64, low, high)
        if block == 0:
            loads[1].wait()
            loads[2].wait()
        lanes = pl.ds(block * LANES, LANES)
        seen = gathered[...].T
        contact[:, lanes] = seen
        own = wall[:, lanes]
        out[:, :, :, lanes] = (
            own + MIXING_WEIGHT * (film[:, lanes] * (seen - own))
        ).reshape(2, 8, 8, LANES)
        copies = [
            pltpu.make_async_copy(
                contact.at[:, lanes], contact_out.at[:, lanes], out_sems.at[block, 0]
            )
        ] + [
            pltpu.make_async_copy(
                out.at[side, :, :, lanes], t_out.at[:, 7 * side, :, lanes], out_sems.at[block, 1 + side]
            )
            for side in range(2)
        ]
        for copy in copies:
            copy.start()
        stores += copies
    for copy in stores:
        copy.wait()


def vmem():
    return pl.BlockSpec(memory_space=pltpu.VMEM)


def smem():
    return pl.BlockSpec(memory_space=pltpu.SMEM)


def hbm():
    return pl.BlockSpec(memory_space=pltpu.HBM)


def far(array):
    return pltpu.with_memory_space_constraint(array, pltpu.HBM)


def params(mebibytes):
    return pltpu.CompilerParams(vmem_limit_bytes=mebibytes * 1024 * 1024)


def edges(warmth, velocity):
    side = jax.ShapeDtypeStruct((8, 512), jnp.float32)
    return pl.pallas_call(
        edge_kernel,
        out_shape=(side, side),
        in_specs=[hbm(), hbm()],
        out_specs=(vmem(), vmem()),
        scratch_shapes=[
            pltpu.VMEM((2, 2, 512, LANES), jnp.float32),
            pltpu.SemaphoreType.DMA((2, 2)),
        ],
        compiler_params=params(4),
        name="edges",
    )(far(warmth), far(velocity))


def near(array):
    return pltpu.with_memory_space_constraint(array, pltpu.VMEM)


def begin(t, v, owner):
    f32 = jnp.float32
    from_even, from_odd, smoothing, _ = gll_tables()
    count = t.shape[-1]
    return pl.pallas_call(
        functools.partial(begin_kernel, from_even, from_odd),
        out_shape=(
            pltpu.VMEM((8, 8, 8, count), f32),
            pltpu.VMEM((8, 8, 8, count), f32),
            pltpu.VMEM((256, count), f32),
            pltpu.VMEM((256, count), f32),
            pltpu.VMEM((2, 256, 512), jnp.bfloat16),
            jax.ShapeDtypeStruct((16, 128), jnp.int32),
            pltpu.VMEM((4096, LANES), f32),
        ),
        in_specs=[vmem(), hbm(), hbm(), vmem()],
        out_specs=(vmem(),) * 7,
        scratch_shapes=[
            pltpu.VMEM((512, count), jnp.bfloat16),
            pltpu.VMEM((512, count), jnp.bfloat16),
            pltpu.SemaphoreType.DMA((6,)),
        ],
        compiler_params=params(20),
        name="begin",
    )(near(t), far(v), far(jnp.asarray(smoothing)), owner)


def sweeps(v, adv, even, odd, film, smoothing, from_first, from_second, position, cleared):
    f32 = jnp.float32
    bf16 = jnp.bfloat16
    from_even, from_odd, _, _ = gll_tables()
    count = v.shape[-1]
    held = [near(x) for x in (v, adv, even, odd)] + [far(film), near(smoothing)]
    return pl.pallas_call(
        functools.partial(sweep_kernel, from_even, from_odd),
        out_shape=(
            jax.ShapeDtypeStruct((8, 8, 8, count), f32),
            pltpu.HBM((128, count), f32),
            pltpu.VMEM((4096, LANES), f32),
        ),
        in_specs=[vmem()] * 4 + [hbm()] + [vmem()] * 3 + [hbm(), vmem()],
        out_specs=(hbm(), hbm(), vmem()),
        scratch_shapes=[
            pltpu.SMEM((16, 128), jnp.int32),
            pltpu.VMEM((128, count), f32),
            pltpu.VMEM((128, count), f32),
            pltpu.VMEM((8, 8, 8, LANES), f32),
            pltpu.VMEM((8, 8, 8, LANES), f32),
            pltpu.VMEM((2, 8, 8, 8, LANES), f32),
            pltpu.VMEM((512, LANES), bf16),
            pltpu.VMEM((512, LANES), bf16),
            pltpu.VMEM((2, 256, LANES), f32),
            pltpu.VMEM((2, 256, LANES), f32),
            pltpu.VMEM((8, 8, 8, count), f32),
            pltpu.VMEM((8, 8, 8, count), f32),
            pltpu.VMEM((512, count), bf16),
            pltpu.VMEM((512, count), bf16),
            pltpu.VMEM((256, count), f32),
            pltpu.VMEM((256, count), f32),
            pltpu.VMEM((128, 512), f32),
            pltpu.VMEM((2, count, LANES), f32),
            pltpu.SemaphoreType.DMA(()),
            pltpu.SemaphoreType.DMA((6,)),
        ],
        input_output_aliases={9: 2},
        compiler_params=params(28),
        name="sweeps",
    )(*held, from_first, from_second, position, near(cleared))


def plates(arrived, cell, plate_temp, conductivity):
    f32 = jnp.float32
    plate_op = gll_tables()[3]
    return pl.pallas_call(
        owner_kernel,
        out_shape=(
            jax.ShapeDtypeStruct((128, 512), f32),
            jax.ShapeDtypeStruct((2048, LANES), f32),
        ),
        in_specs=[vmem(), vmem(), hbm(), hbm(), hbm()],
        out_specs=(hbm(), vmem()),
        scratch_shapes=[
            pltpu.VMEM((512, 4096), jnp.bfloat16),
            pltpu.VMEM((4096, 256), jnp.bfloat16),
            pltpu.VMEM((128, 512), f32),
            pltpu.VMEM((128, 512), f32),
            pltpu.VMEM((128, 256), jnp.bfloat16),
            pltpu.VMEM((128, 512), f32),
            pltpu.SemaphoreType.DMA((3,)),
            pltpu.SemaphoreType.DMA(()),
        ],
        compiler_params=params(20),
        name="plates",
    )(arrived, cell, far(plate_temp), far(conductivity), far(jnp.asarray(plate_op)))


def finish(returned, position, wall_film, wall, t_new):
    f32 = jnp.float32
    count = wall.shape[1]
    return pl.pallas_call(
        finish_kernel,
        out_shape=(
            jax.ShapeDtypeStruct((8, 8, 8, count), f32),
            jax.ShapeDtypeStruct((128, count), f32),
        ),
        in_specs=[vmem(), vmem(), hbm(), hbm(), hbm()],
        out_specs=(hbm(), hbm()),
        scratch_shapes=[
            pltpu.SMEM((16, 128), jnp.int32),
            pltpu.VMEM((128, count), f32),
            pltpu.VMEM((128, count), f32),
            pltpu.VMEM((4096, LANES), f32),
            pltpu.VMEM((LANES, LANES), f32),
            pltpu.VMEM((128, count), f32),
            pltpu.VMEM((2, 8, 8, count), f32),
            pltpu.SemaphoreType.DMA((3,)),
            pltpu.SemaphoreType.DMA((8, 3)),
        ],
        input_output_aliases={4: 0},
        compiler_params=params(12),
        name="finish",
    )(returned, near(position), far(wall_film), far(wall), t_new)


def shards(warmth, velocity, wall_film, face_owner, plate_temp, conductivity, plate_cell):
    count = warmth.shape[1]
    axes = ("flow", "grp")
    devices = lax.axis_size(axes)

    def exchange(rows):
        return lax.all_to_all(rows, axes, split_axis=0, concat_axis=0, tiled=True)

    to_first, to_second = edges(warmth, velocity)
    pairs = [[(i, i + 1) for i in range(start, devices - 1, 2)] for start in (0, 1)]
    swaps = [forth + [(j, i) for i, j in forth] for forth in pairs]
    from_first = lax.ppermute(to_first, axes, swaps[0])
    from_second = lax.ppermute(to_second, axes, swaps[1])
    t, v = (x.reshape(8, 8, 8, count) for x in (warmth, velocity))
    *started, smoothing, position, cleared = begin(t, v, face_owner.reshape(16, 128))
    t_new, wall, sending = sweeps(
        *started, wall_film, smoothing, from_first, from_second, position, cleared
    )
    cell = plate_cell.reshape(32, LANES)
    arrived = exchange(sending.reshape(128, 32, LANES))
    sheet, returning = plates(arrived, cell, plate_temp, conductivity)
    returned = exchange(returning.reshape(128, 16, LANES)).reshape(2048, LANES)
    coolant, boundary = finish(returned, position, wall_film, wall, t_new)
    return coolant.reshape(512, count), boundary, sheet


def solution(mesh):
    placed = (
        P(None, ("flow", "grp")),
        P(None, ("flow", "grp")),
        P(None, ("flow", "grp")),
        P(("flow", "grp"), None),
        P(None, ("flow", "grp")),
        P(None, ("flow", "grp")),
        P(("flow", "grp")),
    )
    return jax.shard_map(
        shards,
        mesh=mesh,
        in_specs=placed,
        out_specs=(P(None, ("flow", "grp")), P(None, ("flow", "grp")), P(None, ("flow", "grp"))),
        check_vma=False,
    )
```
